128 devices in a mesh: row: 8 (over y, core), col: 16 (over z, x).
Axes of the slice: x: 4, y: 4, z: 4, core: 2. Of those that a mesh axis runs over, the one named last changes fastest.
Arguments:
- queries: bfloat16 [16384, 1024], P(('row', 'col')), may hold values from -3 to 3
- passages: bfloat16 [16384, 1024], P('col', 'row'), may hold values from -3 to 3
- positive: int32 [16384], P('row'), may hold values from 0 to 16383, as said below
Outputs:
- loss: float32 [], replicated
- grad_queries: float32 [16384, 1024], P(('row', 'col'))
- grad_passages: float32 [16384, 1024], P('col', 'row')
The draws below stay inside these ranges and needn't reach their ends.
Inputs may be any that keep to these rules, and one draw needn't show every extreme that they name: A permutation: every passage is the positive of exactly one query.
All inputs are finite; a program needn't handle non-finite values.
Results may differ from the reference program's by a relative error of at most 0.015.
Values may be sent and summed in bfloat16 or wider, within the bound.
No kernel may reach another device: no remote copies, remote signals or barrier semaphores. Data moves between devices by JAX's collectives and lax.ppermute only.
A program may use at most 64 MiB of HBM per device.

```python
import math
import jax
import jax.numpy as jnp
from jax import lax

D = 1024
QUERIES = 16384
Q_BLOCK = 2048
P_BLOCK = 1024
N_ROW = 8
N_COL = 16


def shared(key):
    key_base, key_order = jax.random.split(key)
    base = jax.random.normal(key_base, (QUERIES, D), jnp.float32) * D ** (-0.5)
    order = jax.random.permutation(key_order, QUERIES)
    return (base, order)


def alignment(top_value, low_value):
    place = jnp.arange(QUERIES, dtype=jnp.float32)[:, None] / QUERIES
    aligned = top_value * (1.0 - place) + low_value * place
    return (aligned, jnp.sqrt(1.0 - aligned * aligned))


def draw_queries(key, part):
    base, order = shared(key)
    key = jax.random.fold_in(key, 11)
    key_noise, key_scale = jax.random.split(key)
    noise = jax.random.normal(key_noise, (QUERIES, D), jnp.float32) * D ** (-0.5)
    scales = jnp.exp(jax.random.uniform(key_scale, (QUERIES, 1), jnp.float32, math.log(0.6), math.log(1.6)))
    aligned, rest = alignment(0.75, 0.05)
    values = scales * (aligned * base + rest * noise)
    return jnp.clip(values, -3.0, 3.0).astype(jnp.bfloat16)


def draw_passages(key, part):
    base, order = shared(key)
    key = jax.random.fold_in(key, 23)
    key_noise, key_scale = jax.random.split(key)
    noise = jax.random.normal(key_noise, (QUERIES, D), jnp.float32) * D ** (-0.5)
    scales = jnp.exp(jax.random.uniform(key_scale, (QUERIES, 1), jnp.float32, math.log(0.6), math.log(1.6)))
    values = scales * (0.45 * base + 0.89 * noise)
    inverse = jnp.argsort(order)
    return jnp.clip(values[inverse], -3.0, 3.0).astype(jnp.bfloat16)


def draw_positive(key, part):
    base, order = shared(key)
    return order.astype(jnp.int32)


def setup_inputs(seed: int = 0) -> dict:
    seeds = jax.random.split(jax.random.key(seed), 4)
    return {
        "queries": draw_queries(jax.random.fold_in(seeds[3], 71), 0),
        "passages": draw_passages(jax.random.fold_in(seeds[3], 71), 0),
        "positive": draw_positive(jax.random.fold_in(seeds[3], 71), 0),
    }


logit_scale = 40.0


def scores_of(query_rows, passage_all):
    return logit_scale * jnp.dot(query_rows, passage_all.T, precision=lax.Precision.HIGHEST, preferred_element_type=jnp.float32)


def reference(queries, passages, positive):
    query_all = queries.astype(jnp.float32)
    passage_all = passages.astype(jnp.float32)
    query_blocks = query_all.reshape(N_ROW, Q_BLOCK, D)
    target_blocks = positive.reshape(N_ROW, Q_BLOCK)
    passage_blocks = passage_all.reshape(N_COL, P_BLOCK, D)

    def first_pass(carry, query_rows):
        col_top, col_sum = carry
        scores = scores_of(query_rows, passage_all)
        row_top = jnp.max(scores, axis=1)
        row_lse = row_top + jnp.log(jnp.sum(jnp.exp(scores - row_top[:, None]), axis=1))
        new_top = jnp.maximum(col_top, jnp.max(scores, axis=0))
        col_sum = col_sum * jnp.exp(col_top - new_top) + jnp.sum(jnp.exp(scores - new_top[None, :]), axis=0)
        return (new_top, col_sum), row_lse

    start_top = jnp.full((QUERIES,), -1e30, jnp.float32)
    start_sum = jnp.zeros((QUERIES,), jnp.float32)
    (col_top, col_sum), row_lse = lax.scan(first_pass, (start_top, start_sum), query_blocks)
    col_lse = col_top + jnp.log(col_sum)
    col_ids = jnp.arange(QUERIES, dtype=jnp.int32)

    def second_pass(carry, inputs):
        passage_grad, loss_part = carry
        query_rows, targets, lse_rows = inputs
        scores = scores_of(query_rows, passage_all)
        onehot = (col_ids[None, :] == targets[:, None]).astype(jnp.float32)
        slope = 0.5 * jnp.exp(scores - lse_rows[:, None]) + 0.5 * jnp.exp(scores - col_lse[None, :]) - onehot
        slope = lax.optimization_barrier(slope.astype(jnp.bfloat16)).astype(jnp.float32)
        loss_part = loss_part + jnp.sum(onehot * (lse_rows[:, None] + col_lse[None, :] - 2.0 * scores))
        partial_terms = logit_scale * jnp.einsum("bcj,cjd->cbd", slope.reshape(Q_BLOCK, N_COL, P_BLOCK), passage_blocks, precision=lax.Precision.HIGHEST)
        partial_terms = lax.optimization_barrier(partial_terms.astype(jnp.bfloat16)).astype(jnp.float32)
        query_grad = jnp.sum(partial_terms, axis=0)
        passage_term = logit_scale * jnp.dot(slope.T, query_rows, precision=lax.Precision.HIGHEST)
        passage_term = lax.optimization_barrier(passage_term.astype(jnp.bfloat16)).astype(jnp.float32)
        return (passage_grad + passage_term, loss_part), query_grad

    start_grad = jnp.zeros((QUERIES, D), jnp.float32)
    start_loss = jnp.zeros((), jnp.float32)
    (passage_grad, loss_part), query_grads = lax.scan(second_pass, (start_grad, start_loss), (query_blocks, target_blocks, row_lse))
    loss = loss_part / (2.0 * QUERIES)
    return (loss, query_grads.reshape(QUERIES, D), passage_grad)
```

```python
import functools

import jax
import jax.numpy as jnp
from jax import lax
from jax.experimental import pallas as pl
from jax.experimental.pallas import tpu as pltpu
from jax.sharding import PartitionSpec as P

logit_scale = 40.0
low = -1e30
AX = ("row", "col")
f32, bf16 = jnp.float32, jnp.bfloat16
MIB = 1024 * 1024


def lin(y, c, z, x):
    return ((y * 2 + c) * 4 + z) * 4 + x


def moves(step):
    pairs = []
    for y in range(4):
        for z in range(4):
            for x in range(4):
                pairs.append((lin(y, 0, z, x), lin(y, 0, *step(z, x, x ^ 1))))
                far_y, far_x = step(y, x, 3 - x)
                pairs.append((lin(y, 1, z, x), lin(far_y, 1, z, far_x)))
    return pairs


def hop(a, d, flip):
    return lax.ppermute(a, AX, moves(lambda r, x, other: ((r + d) % 4, other if flip else x)))


def hop_xor(a):
    return lax.ppermute(a, AX, moves(lambda r, x, other: (r ^ 1, x)))


def swap(a):
    return lax.ppermute(a, "row", [(i, i ^ 1) for i in range(8)])


def place():
    row, col = lax.axis_index("row"), lax.axis_index("col")
    return row // 2, row % 2, col // 4, col % 4


OFFSETS = [(0, 0), (0, 1), (1, 0), (3, 0), (2, 0), (1, 1), (3, 1), (2, 1)]


def load_copies(core, y, z, x, mine, theirs, q_dst, p_dst, sems):
    out = []
    for k, (d, flip) in enumerate(OFFSETS):
        slot = ((x % 2) ^ flip) * 4 + (z - d + 4) % 4
        far_y = (y - d + 4) % 4
        rank = (x // 2) ^ flip
        for which in range(2):
            copies = []
            q_src, p_src = (mine[k], theirs[k]) if which == 0 else (theirs[k], mine[k])
            if q_dst is not None:
                rows = pl.ds(pl.multiple_of(slot * 128, 128), 128)
                copies.append(pltpu.make_async_copy(q_src.at[which], q_dst.at[rows], sems.at[k, 0]))
            if p_dst is not None:
                for part in range(2):
                    rows = pl.ds(pl.multiple_of(far_y * 256 + (1 - part) * 128, 128), 128)
                    copies.append(
                        pltpu.make_async_copy(p_src.at[part], p_dst.at[rank, rows], sems.at[k, 1 + part])
                    )
            out.append((which, copies))
    return out


def run_copies(core, groups, start):
    for which in range(2):

        @pl.when(core == which)
        def _():
            for w, copies in groups:
                if w == which:
                    for copy in copies:
                        copy.start() if start else copy.wait()


TILE = 16


def score_kernel(*refs):
    mine, theirs, (target, scores_out, keep, send, qv, pt, sv, row_top, row_sum, col_top, sems, out_sem) = (
        refs[:8],
        refs[8:16],
        refs[16:],
    )
    y, core, z, x = place()
    groups = load_copies(core, y, z, x, mine, theirs, qv, pt, sems)
    run_copies(core, groups, True)
    run_copies(core, groups, False)
    for h in range(2):
        for n in range(4):
            cols = slice(n * 256, n * 256 + 256)
            s = logit_scale * jnp.dot(qv[...], pt[h, :, cols], preferred_element_type=f32)
            sv[h, :, cols] = s
            col_top[:, h * 1024 + n * 256 : h * 1024 + n * 256 + 256] = jnp.broadcast_to(
                jnp.max(s, axis=0, keepdims=True), (8, 256)
            )
    write = pltpu.make_async_copy(sv, scores_out, out_sem)
    write.start()
    lanes = lax.broadcasted_iota(jnp.int32, (TILE, 1024), 1)

    def step(i, carry):
        col_acc, hit_acc = carry
        rows = pl.ds(pl.multiple_of(i * TILE, TILE), TILE)
        parts = [sv[h, rows, :] for h in range(2)]
        aim = target[rows, :1]
        top = jnp.maximum(
            jnp.max(parts[0], axis=1, keepdims=True), jnp.max(parts[1], axis=1, keepdims=True)
        )
        total = jnp.zeros((TILE, 1), f32)
        cols, hits = [], jnp.zeros((TILE, 1024), f32)
        for h in range(2):
            t = parts[h]
            total = total + jnp.sum(jnp.exp(t - top), axis=1, keepdims=True)
            e = jnp.exp(t - col_top[:1, h * 1024 : h * 1024 + 1024])
            cols.append(sum(e[r : r + 8] for r in range(0, TILE, 8)))
            hits = hits + jnp.where(lanes == aim - h * 1024, t, 0.0)
        row_top[rows, :] = jnp.broadcast_to(top, (TILE, 128))
        row_sum[rows, :] = jnp.broadcast_to(total, (TILE, 128))
        hit_acc = hit_acc + sum(hits[r : r + 8] for r in range(0, TILE, 8))
        return (col_acc[0] + cols[0], col_acc[1] + cols[1]), hit_acc

    zero = jnp.zeros((8, 1024), f32)
    col_acc, hit_acc = lax.fori_loop(0, 1024 // TILE, step, ((zero, zero), zero))
    hits = jnp.sum(hit_acc, axis=0, keepdims=True)

    def fill(rows_ref, cols_ref, first):
        off = 0 if first else 1024
        for s in range(8):
            at = slice(off + s * 128, off + s * 128 + 128)
            rows_ref[0:1, at] = row_top[s * 128 : s * 128 + 128, :].T[0:1]
            rows_ref[1:2, at] = row_sum[s * 128 : s * 128 + 128, :].T[0:1]
        gap = slice(1024 - off, 2048 - off)
        rows_ref[0:1, gap] = jnp.full((1, 1024), low, f32)
        rows_ref[1:2, gap] = jnp.zeros((1, 1024), f32)
        rows_ref[2:3, :1024] = hits
        rows_ref[2:3, 1024:] = jnp.zeros((1, 1024), f32)
        cols_ref[0:1, :] = col_top[0:1, :]
        for h in range(2):
            cols_ref[1:2, h * 1024 : h * 1024 + 1024] = jnp.sum(col_acc[h], axis=0, keepdims=True)
        cols_ref[2:3, :] = jnp.zeros((1, 2048), f32)

    @pl.when(core == 0)
    def _():
        fill(keep, send, True)

    @pl.when(core == 1)
    def _():
        fill(send, keep, False)

    write.wait()


def flip_kernel(*refs):
    mine, theirs, (_, out, qv, sems) = refs[:8], refs[8:16], refs[16:]
    y, core, z, x = place()
    groups = load_copies(core, y, z, x, mine, theirs, qv, None, sems)
    run_copies(core, groups, True)
    run_copies(core, groups, False)
    for m in range(8):
        out[:, m * 128 : m * 128 + 128] = qv[m * 128 : m * 128 + 128, :].T


def grad_kernel(flip, order, with_slope, *refs):
    n = len(order)
    mine, theirs, refs = refs[:8], refs[8:16], refs[16:]
    if with_slope:
        (scores, target, own_lse, got_lse, q_flip), refs = refs[:5], refs[5:]
        keeps, sends, slope_out, refs = refs[:n], refs[n : 2 * n], refs[2 * n], refs[2 * n + 1 :]
        (pt, qt, slope, gq, gp, zeros, sems, in_sem, q_sem, out_sems, sl_sem, sv, row_lse) = refs
    else:
        (slope_in, q_flip), refs = refs[:2], refs[2:]
        keeps, sends, refs = refs[:n], refs[n : 2 * n], refs[2 * n :]
        (pt, qt, slope, gq, gp, zeros, sems, in_sem, q_sem, out_sems) = refs
    y, core, z, x = place()
    groups = load_copies(core, y, z, x, mine, theirs, None, pt, sems)
    q_copy = pltpu.make_async_copy(q_flip, qt, q_sem)
    zeros[...] = jnp.zeros(zeros.shape, bf16)
    if with_slope:
        reads = [
            pltpu.make_async_copy(
                scores.at[:, pl.ds(s * 128, 128)], sv.at[:, pl.ds(s * 128, 128)], in_sem.at[s]
            )
            for s in range(8)
        ]
        for read in reads:
            read.start()
        q_copy.start()
        run_copies(core, groups, True)
        first = core == 0
        mine_lse, their_lse = own_lse[...], got_lse[...]
        rows_lse = jnp.where(first, mine_lse[:, :1024], their_lse[:, 1024:])
        cols_lse = jnp.where(first, their_lse, mine_lse)
        for s in range(8):
            row_lse[s * 128 : s * 128 + 128, :] = jnp.broadcast_to(
                rows_lse[:, s * 128 : s * 128 + 128], (128, 128)
            ).T
        lanes = lax.broadcasted_iota(jnp.int32, (TILE, 1024), 1)

        for s in range(8):
            reads[s].wait()

            def step(i, carry, s=s):
                rows = pl.ds(pl.multiple_of(s * 128 + i * TILE, TILE), TILE)
                aim = target[rows, :1]
                lse = row_lse[rows, :1]
                for h in range(2):
                    t = sv[h, rows, :]
                    e = 0.5 * jnp.exp(t - lse) + 0.5 * jnp.exp(t - cols_lse[:, h * 1024 : h * 1024 + 1024])
                    e = e - jnp.where(lanes == aim - h * 1024, 1.0, 0.0)
                    slope[h, rows, :] = e.astype(bf16)
                return carry

            lax.fori_loop(0, 128 // TILE, step, 0)
        slope_copy = pltpu.make_async_copy(slope, slope_out, sl_sem)
        slope_copy.start()
    else:
        slope_copy = pltpu.make_async_copy(slope_in, slope, in_sem.at[0])
        slope_copy.start()
        q_copy.start()
        run_copies(core, groups, True)
        slope_copy.wait()
    run_copies(core, groups, False)
    half = (x % 2) ^ flip
    rank = (x // 2) ^ flip
    rows = pl.ds(pl.multiple_of(half * 512, 512), 512)
    for m in range(4):
        cut = slice(m * 256, m * 256 + 256)
        g = sum(
            lax.dot_general(
                slope[h, rows, :], pt[h, cut, :], (((1,), (1,)), ((), ())), preferred_element_type=f32
            )
            for h in range(2)
        )
        gq[:, cut] = (logit_scale * g).astype(bf16)
    q_copy.wait()
    for m in range(4):
        cut = slice(m * 256, m * 256 + 256)
        g = jnp.dot(qt[...], slope[rank, :, cut], preferred_element_type=f32)
        gp[:, cut] = (logit_scale * g).astype(bf16)

    def outs(which):
        copies = []
        for k, d in enumerate(order):
            q_rows = pl.ds(pl.multiple_of((z + d) % 4 * 128, 128), 128)
            far_y = (y + d) % 4
            q_from = gq.at[q_rows]
            p_to, q_to = (sends[k], keeps[k]) if which == 0 else (keeps[k], sends[k])
            for part in range(2):
                p_rows = pl.ds(pl.multiple_of(far_y * 256 + (1 - part) * 128, 128), 128)
                copies.append(pltpu.make_async_copy(gp.at[p_rows], p_to.at[part], out_sems.at[k, part]))
            copies.append(pltpu.make_async_copy(q_from, q_to.at[which], out_sems.at[k, 2]))
            copies.append(pltpu.make_async_copy(zeros, q_to.at[1 - which], out_sems.at[k, 3]))
        return copies

    for which in range(2):

        @pl.when(core == which)
        def _():
            copies = outs(which)
            for copy in copies:
                copy.start()
            for copy in copies:
                copy.wait()

    if with_slope:
        slope_copy.wait()


ANY = pl.BlockSpec(memory_space=pl.ANY)
VM = pl.BlockSpec(memory_space=pltpu.VMEM)


def arr(shape, dtype):
    return jax.ShapeDtypeStruct(shape, dtype)


def cost(flops, nbytes):
    return pl.CostEstimate(flops=flops, bytes_accessed=nbytes, transcendentals=0)


def scores_of(mine, theirs, target):
    return pl.pallas_call(
        score_kernel,
        out_shape=(arr((2, 1024, 1024), f32), arr((3, 2048), f32), arr((3, 2048), f32)),
        in_specs=[ANY] * 16 + [VM],
        out_specs=(ANY, VM, VM),
        scratch_shapes=[
            pltpu.VMEM((1024, 1024), bf16),
            pltpu.VMEM((2, 1024, 1024), bf16),
            pltpu.VMEM((2, 1024, 1024), f32),
            pltpu.VMEM((1024, 128), f32),
            pltpu.VMEM((1024, 128), f32),
            pltpu.VMEM((8, 2048), f32),
            pltpu.SemaphoreType.DMA((8, 3)),
            pltpu.SemaphoreType.DMA,
        ],
        compiler_params=pltpu.CompilerParams(vmem_limit_bytes=40 * MIB),
        cost_estimate=cost(2 * 1024**2 * 2048, 16 * MIB),
        name="scores",
    )(*mine, *theirs, target)


def flipped(mine, theirs, after):
    return pl.pallas_call(
        flip_kernel,
        out_shape=arr((1024, 1024), bf16),
        in_specs=[ANY] * 17,
        out_specs=VM,
        scratch_shapes=[pltpu.VMEM((1024, 1024), bf16), pltpu.SemaphoreType.DMA((8, 3))],
        compiler_params=pltpu.CompilerParams(vmem_limit_bytes=16 * MIB),
        cost_estimate=cost(0, 4 * MIB),
        name="flip",
    )(*mine, *theirs, after)


def grads_of(flip, order, mine, theirs, operands, in_specs, with_slope):
    n = len(order)
    chunk = arr((2, 128, 1024), bf16)
    out_shape = [chunk] * (2 * n) + ([arr((2, 1024, 1024), bf16)] if with_slope else [])
    scratch = [
        pltpu.VMEM((2, 1024, 1024), bf16),
        pltpu.VMEM((1024, 1024), bf16),
        pltpu.VMEM((2, 1024, 1024), bf16),
        pltpu.VMEM((512, 1024), bf16),
        pltpu.VMEM((1024, 1024), bf16),
        pltpu.VMEM((128, 1024), bf16),
        pltpu.SemaphoreType.DMA((8, 3)),
        pltpu.SemaphoreType.DMA((8,)),
        pltpu.SemaphoreType.DMA,
        pltpu.SemaphoreType.DMA((n, 4)),
    ]
    if with_slope:
        scratch += [
            pltpu.SemaphoreType.DMA,
            pltpu.VMEM((2, 1024, 1024), f32),
            pltpu.VMEM((1024, 128), f32),
        ]
    return pl.pallas_call(
        functools.partial(grad_kernel, flip, order, with_slope),
        out_shape=out_shape,
        in_specs=[ANY] * 16 + in_specs,
        out_specs=[ANY] * len(out_shape),
        scratch_shapes=scratch,
        compiler_params=pltpu.CompilerParams(vmem_limit_bytes=48 * MIB),
        cost_estimate=cost(2 * 1024**2 * 2048, 20 * MIB),
        name="grads_far" if flip else "grads_near",
    )(*mine, *theirs, *operands)


def merge(a, b):
    top = jnp.maximum(a[0], b[0])
    total = a[1] * jnp.exp(a[0] - top) + b[1] * jnp.exp(b[0] - top)
    return jnp.stack([top, total, a[2] + b[2]])


def shards(queries, passages, positive):
    y, core, z, x = place()
    first = core == 0
    flat = passages.T
    got = swap(jnp.where(first, flat, queries))
    own = jnp.stack([jnp.where(first, queries, flat), got])
    across = hop(own, 0, True)
    up, down, far = hop(own, 1, False), hop(own, 3, False), hop(own, 2, False)
    chunks = [own, across, up, down, far, hop(up, 0, True), hop(down, 0, True), hop(across, 2, False)]
    others = [swap(c) for c in chunks]

    aims = positive.reshape(4, 2, 2, 128)
    aims = jnp.where(x // 2 == 0, aims[:, 0], aims[:, 1]).transpose(1, 0, 2).reshape(1024)
    block = aims // 1024
    in_tile = (block // 4 == z) & ((block % 4 + 1) % 4 // 2 == (x + 1) % 4 // 2)
    aims = jnp.where(in_tile, block % 4 // 2 * 1024 + aims % 1024, -1)
    aims = jnp.broadcast_to(aims[:, None], (1024, 128))

    scores, keep, send = scores_of(chunks, others, aims)
    q_flip = flipped(chunks, others, keep)
    stats = merge(keep, swap(send))
    stats = merge(stats, hop(stats, 0, True))
    stats = merge(stats, hop_xor(stats))
    stats = merge(stats, hop(stats, 2, False))
    own_lse = (stats[0] + jnp.log(stats[1])).reshape(1, 2048)
    got_lse = swap(own_lse)

    far_order, near_order = (1, 3, 2, 0), (1, 3, 2, 0)
    outs = grads_of(1, far_order, chunks, others, (scores, aims, own_lse, got_lse, q_flip), [ANY, VM, VM, VM, ANY], True)
    keeps, sends, slope = outs[:4], outs[4:8], outs[8]

    def add(a, b):
        return (a.astype(f32) + b.astype(f32)).astype(bf16)

    total = []
    for d, k, s in zip(far_order, keeps, sends):
        total.append(hop(add(k, swap(s)), d, True))
    outs = grads_of(0, near_order, chunks, others, (slope, q_flip), [ANY, ANY], False)
    for d, k, s in zip(near_order, outs[:4], outs[4:]):
        part = add(k, swap(s))
        total.append(hop(part, d, False) if d else part)
    grads = sum(t.astype(f32) for t in total)
    other = swap(grads[1])
    grad_queries = jnp.where(first, grads[0], other)
    grad_passages = jnp.where(first, other, grads[0]).T

    part = jnp.sum(own_lse) - 2.0 * jnp.sum(stats[2])
    part = swap(part)
    part = part + hop(part, 0, True)
    part = part + hop_xor(part)
    part = part + hop(part, 2, False)
    loss = (part + swap(part)) / 32768.0
    return loss, grad_queries, grad_passages


def solution(mesh):
    in_specs = (P(("row", "col"), None), P("col", "row"), P("row"))
    out_specs = (P(), P(("row", "col"), None), P("col", "row"))
    return jax.shard_map(shards, mesh=mesh, in_specs=in_specs, out_specs=out_specs, check_vma=False)
```

```python
import functools

import jax
import jax.numpy as jnp
from jax import lax
from jax.experimental import pallas as pl
from jax.experimental.pallas import tpu as pltpu
from jax.sharding import PartitionSpec as P

logit_scale = 40.0
log2_e = 1.4426950408889634
score_scale = logit_scale * log2_e
low = -1e30
AX = ("row", "col")
f32, bf16 = jnp.float32, jnp.bfloat16
MIB = 1024 * 1024


def lin(y, c, z, x):
    return ((y * 2 + c) * 4 + z) * 4 + x


def moves(step):
    pairs = []
    for y in range(4):
        for z in range(4):
            for x in range(4):
                pairs.append((lin(y, 0, z, x), lin(y, 0, *step(z, x, x ^ 1))))
                far_y, far_x = step(y, x, 3 - x)
                pairs.append((lin(y, 1, z, x), lin(far_y, 1, z, far_x)))
    return pairs


def hop(a, d, flip):
    return lax.ppermute(a, AX, moves(lambda r, x, other: ((r + d) % 4, other if flip else x)))


def hop_xor(a):
    return lax.ppermute(a, AX, moves(lambda r, x, other: (r ^ 1, x)))


def swap(a):
    return lax.ppermute(a, "row", [(i, i ^ 1) for i in range(8)])


def place():
    row, col = lax.axis_index("row"), lax.axis_index("col")
    return row // 2, row % 2, col // 4, col % 4


OFFSETS = [(0, 0), (0, 1), (1, 0), (3, 0), (2, 0), (1, 1), (3, 1), (2, 1)]


def load_copies(core, y, z, x, mine, theirs, q_dst, p_dst, sems):
    out = []
    for k, (d, flip) in enumerate(OFFSETS):
        slot = ((x % 2) ^ flip) * 4 + (z - d + 4) % 4
        far_y = (y - d + 4) % 4
        rank = (x // 2) ^ flip
        for which in range(2):
            copies = []
            q_src, p_src = (mine[k], theirs[k]) if which == 0 else (theirs[k], mine[k])
            if q_dst is not None:
                rows = pl.ds(pl.multiple_of(slot * 128, 128), 128)
                copies.append(pltpu.make_async_copy(q_src.at[which], q_dst.at[rows], sems.at[k, 0]))
            if p_dst is not None:
                for part in range(2):
                    rows = pl.ds(pl.multiple_of(far_y * 256 + (1 - part) * 128, 128), 128)
                    copies.append(
                        pltpu.make_async_copy(p_src.at[part], p_dst.at[rank, rows], sems.at[k, 1 + part])
                    )
            out.append((which, copies))
    return out


def run_copies(core, groups, start):
    for which in range(2):

        @pl.when(core == which)
        def _():
            for w, copies in groups:
                if w == which:
                    for copy in copies:
                        copy.start() if start else copy.wait()


TILE = 32


def lane_groups():
    return [(g // 8, slice(g % 8 * 128, g % 8 * 128 + 128)) for g in range(16)]


def fold(a):
    return sum(a[r : r + 8] for r in range(0, a.shape[0], 8))


def score_kernel(*refs):
    mine, theirs, (target, sv, keep, send, qv, pt, row_top, row_sum, col_top, sems) = (
        refs[:8],
        refs[8:16],
        refs[16:],
    )
    y, core, z, x = place()
    groups = load_copies(core, y, z, x, mine, theirs, qv, pt, sems)
    run_copies(core, groups, True)
    run_copies(core, groups, False)
    for h in range(2):
        for n in range(2):
            cols = slice(n * 512, n * 512 + 512)
            s = score_scale * jnp.dot(qv[...], pt[h, :, cols], preferred_element_type=f32)
            sv[h, :, cols] = s
            col_top[h, :, cols] = jnp.broadcast_to(jnp.max(s, axis=0, keepdims=True), (8, 512))
            top = jnp.maximum(
                jnp.maximum(s[:, :128], s[:, 128:256]), jnp.maximum(s[:, 256:384], s[:, 384:])
            )
            row_top[...] = top if h == n == 0 else jnp.maximum(row_top[...], top)
    tops = []
    for s in range(8):
        rows = slice(s * 128, s * 128 + 128)
        top = jnp.max(row_top[rows, :].T, axis=0, keepdims=True)
        tops.append(top)
        row_top[rows, :] = jnp.broadcast_to(top, (128, 128)).T
    lanes = lax.broadcasted_iota(jnp.int32, (TILE, 128), 1)

    def step(i, carry):
        col_acc, hits = carry
        rows = pl.ds(pl.multiple_of(i * TILE, TILE), TILE)
        top, aim = row_top[rows, :], target[rows, :]
        total, cols = jnp.zeros((TILE, 128), f32), []
        for g, (h, at) in enumerate(lane_groups()):
            t = sv[h, rows, at]
            total = total + jnp.exp2(t - top)
            cols.append(col_acc[g] + fold(jnp.exp2(t - col_top[h, 0:1, at])))
            hits = hits + fold(jnp.where(lanes == aim - g * 128, t, 0.0))
        row_sum[rows, :] = total
        return tuple(cols), hits

    zero = jnp.zeros((8, 128), f32)
    col_acc, hits = lax.fori_loop(0, 1024 // TILE, step, ((zero,) * 16, zero))
    hits = jnp.sum(hits, axis=0, keepdims=True)

    def fill(rows_ref, cols_ref, first):
        off = 0 if first else 1024
        for s in range(8):
            at = slice(off + s * 128, off + s * 128 + 128)
            rows_ref[0:1, at] = tops[s]
            rows_ref[1:2, at] = jnp.sum(row_sum[s * 128 : s * 128 + 128, :].T, axis=0, keepdims=True)
        gap = slice(1024 - off, 2048 - off)
        rows_ref[0:1, gap] = jnp.full((1, 1024), low, f32)
        rows_ref[1:2, gap] = jnp.zeros((1, 1024), f32)
        rows_ref[2:3, :] = jnp.zeros((1, 2048), f32)
        rows_ref[2:3, :128] = hits
        for h in range(2):
            cols_ref[0:1, h * 1024 : h * 1024 + 1024] = col_top[h, 0:1, :]
        for g in range(16):
            cols_ref[1:2, g * 128 : g * 128 + 128] = jnp.sum(col_acc[g], axis=0, keepdims=True)
        cols_ref[2:3, :] = jnp.zeros((1, 2048), f32)

    @pl.when(core == 0)
    def _():
        fill(keep, send, True)

    @pl.when(core == 1)
    def _():
        fill(send, keep, False)


def flip_kernel(*refs):
    mine, theirs, (_, out, qv, sems) = refs[:8], refs[8:16], refs[16:]
    y, core, z, x = place()
    groups = load_copies(core, y, z, x, mine, theirs, qv, None, sems)
    run_copies(core, groups, True)
    run_copies(core, groups, False)
    for m in range(8):
        out[:, m * 128 : m * 128 + 128] = qv[m * 128 : m * 128 + 128, :].T


def grad_kernel(flip, order, with_slope, n_ties, *refs):
    n = len(order)
    mine, theirs, refs = refs[:8], refs[8:16], refs[16:]
    steps = [(g, i, d) for g, group in enumerate(order) for i, d in enumerate(group)]
    if with_slope:
        (sv, target, own_lse, got_lse, q_flip), refs = refs[:5], refs[5 + n_ties :]
        keeps, sends, slope_out, refs = refs[:n], refs[n : 2 * n], refs[2 * n], refs[2 * n + 1 :]
        (pt, qt, slope, gq, gp, zeros, sems, in_sem, q_sem, out_sems, sl_sem, row_lse) = refs
    else:
        (slope_in, q_flip), refs = refs[:2], refs[2 + n_ties :]
        keeps, sends, refs = refs[:n], refs[n : 2 * n], refs[2 * n :]
        (pt, qt, slope, gq, gp, zeros, sems, in_sem, q_sem, out_sems) = refs
    y, core, z, x = place()
    groups = load_copies(core, y, z, x, mine, theirs, None, pt, sems)
    q_copy = pltpu.make_async_copy(q_flip, qt, q_sem)
    zeros[...] = jnp.zeros(zeros.shape, bf16)
    if with_slope:
        q_copy.start()
        run_copies(core, groups, True)
        first = core == 0
        mine_lse, their_lse = own_lse[...], got_lse[...]
        rows_lse = jnp.where(first, mine_lse[:, :1024], their_lse[:, 1024:])
        cols_lse = jnp.where(first, their_lse, mine_lse)
        for s in range(8):
            row_lse[s * 128 : s * 128 + 128, :] = jnp.broadcast_to(
                rows_lse[:, s * 128 : s * 128 + 128], (128, 128)
            ).T
        lanes = lax.broadcasted_iota(jnp.int32, (TILE, 128), 1)

        def step(i, carry):
            rows = pl.ds(pl.multiple_of(i * TILE, TILE), TILE)
            aim, lse = target[rows, :], row_lse[rows, :]
            for g, (h, at) in enumerate(lane_groups()):
                t = sv[h, rows, at]
                e = 0.5 * (jnp.exp2(t - lse) + jnp.exp2(t - cols_lse[:, g * 128 : g * 128 + 128]))
                slope[h, rows, at] = jnp.where(lanes == aim - g * 128, e - 1.0, e).astype(bf16)
            return carry

        lax.fori_loop(0, 1024 // TILE, step, 0)
        slope_copy = pltpu.make_async_copy(slope, slope_out, sl_sem)
        slope_copy.start()
    else:
        slope_copy = pltpu.make_async_copy(slope_in, slope, in_sem.at[0])
        slope_copy.start()
        q_copy.start()
        run_copies(core, groups, True)
        slope_copy.wait()
    run_copies(core, groups, False)
    half = (x % 2) ^ flip
    rank = (x // 2) ^ flip
    rows = pl.ds(pl.multiple_of(half * 512, 512), 512)
    for m in range(4):
        cut = slice(m * 256, m * 256 + 256)
        g = sum(
            lax.dot_general(
                slope[h, rows, :], pt[h, cut, :], (((1,), (1,)), ((), ())), preferred_element_type=f32
            )
            for h in range(2)
        )
        gq[:, cut] = (logit_scale * g).astype(bf16)
    q_copy.wait()
    for m in range(4):
        cut = slice(m * 256, m * 256 + 256)
        g = jnp.dot(qt[...], slope[rank, :, cut], preferred_element_type=f32)
        gp[:, cut] = (logit_scale * g).astype(bf16)

    def outs(which):
        copies = []
        for k, (g, i, d) in enumerate(steps):
            q_rows = pl.ds(pl.multiple_of((z + d) % 4 * 128, 128), 128)
            far_y = (y + d) % 4
            q_from = gq.at[q_rows]
            p_to, q_to = (sends[g], keeps[g]) if which == 0 else (keeps[g], sends[g])
            p_to, q_to = p_to.at[i], q_to.at[i]
            for part in range(2):
                p_rows = pl.ds(pl.multiple_of(far_y * 256 + (1 - part) * 128, 128), 128)
                copies.append(pltpu.make_async_copy(gp.at[p_rows], p_to.at[part], out_sems.at[k, part]))
            copies.append(pltpu.make_async_copy(q_from, q_to.at[which], out_sems.at[k, 2]))
            copies.append(pltpu.make_async_copy(zeros, q_to.at[1 - which], out_sems.at[k, 3]))
        return copies

    for which in range(2):

        @pl.when(core == which)
        def _():
            copies = outs(which)
            for copy in copies:
                copy.start()
            for copy in copies:
                copy.wait()

    if with_slope:
        slope_copy.wait()


ANY = pl.BlockSpec(memory_space=pl.ANY)
VM = pl.BlockSpec(memory_space=pltpu.VMEM)


def arr(shape, dtype):
    return jax.ShapeDtypeStruct(shape, dtype)


def cost(flops, nbytes):
    return pl.CostEstimate(flops=flops, bytes_accessed=nbytes, transcendentals=0)


def scores_of(mine, theirs, target):
    return pl.pallas_call(
        score_kernel,
        out_shape=(arr((2, 1024, 1024), f32), arr((3, 2048), f32), arr((3, 2048), f32)),
        in_specs=[ANY] * 16 + [VM],
        out_specs=(VM, VM, VM),
        scratch_shapes=[
            pltpu.VMEM((1024, 1024), bf16),
            pltpu.VMEM((2, 1024, 1024), bf16),
            pltpu.VMEM((1024, 128), f32),
            pltpu.VMEM((1024, 128), f32),
            pltpu.VMEM((2, 8, 1024), f32),
            pltpu.SemaphoreType.DMA((8, 3)),
        ],
        compiler_params=pltpu.CompilerParams(vmem_limit_bytes=32 * MIB),
        cost_estimate=cost(2 * 1024**2 * 2048, 16 * MIB),
        name="scores",
    )(*mine, *theirs, target)


def flipped(mine, theirs, after):
    return pl.pallas_call(
        flip_kernel,
        out_shape=arr((1024, 1024), bf16),
        in_specs=[ANY] * 17,
        out_specs=VM,
        scratch_shapes=[pltpu.VMEM((1024, 1024), bf16), pltpu.SemaphoreType.DMA((8, 3))],
        compiler_params=pltpu.CompilerParams(vmem_limit_bytes=16 * MIB),
        cost_estimate=cost(0, 4 * MIB),
        name="flip",
    )(*mine, *theirs, after)


def grads_of(flip, order, mine, theirs, operands, in_specs, with_slope, ties=()):
    n = len(order)
    chunks = [arr((len(group), 2, 128, 1024), bf16) for group in order]
    out_shape = chunks * 2 + ([arr((2, 1024, 1024), bf16)] if with_slope else [])
    scratch = [
        pltpu.VMEM((2, 1024, 1024), bf16),
        pltpu.VMEM((1024, 1024), bf16),
        pltpu.VMEM((2, 1024, 1024), bf16),
        pltpu.VMEM((512, 1024), bf16),
        pltpu.VMEM((1024, 1024), bf16),
        pltpu.VMEM((128, 1024), bf16),
        pltpu.SemaphoreType.DMA((8, 3)),
        pltpu.SemaphoreType.DMA((8,)),
        pltpu.SemaphoreType.DMA,
        pltpu.SemaphoreType.DMA((4, 4)),
    ]
    if with_slope:
        scratch += [
            pltpu.SemaphoreType.DMA,
            pltpu.VMEM((1024, 128), f32),
        ]
    return pl.pallas_call(
        functools.partial(grad_kernel, flip, order, with_slope, len(ties)),
        out_shape=out_shape,
        in_specs=[ANY] * 16 + in_specs + [ANY] * len(ties),
        out_specs=[ANY] * len(out_shape),
        scratch_shapes=scratch,
        compiler_params=pltpu.CompilerParams(vmem_limit_bytes=32 * MIB),
        cost_estimate=cost(2 * 1024**2 * 2048, 20 * MIB),
        name="grads_far" if flip else "grads_near",
    )(*mine, *theirs, *operands, *ties)


def join_kernel(picks, *refs):
    out = refs[-1]
    parts = [r[...] if p is None else r[p : p + 1] for p, r in zip(picks, refs)]
    out[...] = sum(p.astype(f32) for p in parts).astype(bf16)


def join(terms, ties=(), pick=None):
    a, n = terms[0], len(terms)
    return pl.pallas_call(
        functools.partial(join_kernel, [None] * (n - 1) + [pick]),
        out_shape=arr(a.shape, bf16),
        in_specs=[VM] * n + [ANY] * len(ties),
        out_specs=VM,
        compiler_params=pltpu.CompilerParams(vmem_limit_bytes=16 * MIB),
        cost_estimate=cost(a.size, 6 * a.size),
        name="join",
    )(*terms, *ties)


def total_kernel(n, *refs):
    mine, other = refs[-2:]
    mine[...] = sum(r[0, 0].astype(f32) for r in refs[:n])
    other[...] = sum(r[0, 1].astype(f32) for r in refs[:n])


def total(terms, ties=()):
    return pl.pallas_call(
        functools.partial(total_kernel, len(terms)),
        out_shape=[arr((128, 1024), f32)] * 2,
        in_specs=[VM] * len(terms) + [ANY] * len(ties),
        out_specs=[VM] * 2,
        compiler_params=pltpu.CompilerParams(vmem_limit_bytes=16 * MIB),
        cost_estimate=cost(5 * 2**18, 4 * MIB),
        name="total",
    )(*terms, *ties)


def merge_kernel(last, a, b, *refs):
    top = jnp.maximum(a[0:1], b[0:1])
    total = a[1:2] * jnp.exp2(a[0:1] - top) + b[1:2] * jnp.exp2(b[0:1] - top)
    hits = a[2:3] + b[2:3]
    if last:
        lse, part = refs[-2:]
        lse[...] = top + jnp.log2(total)
        figure = jnp.sum(lse[...] - 2.0 * hits, axis=1, keepdims=True)
        part[...] = jnp.broadcast_to(figure, (8, 128))
    else:
        out = refs[-1]
        out[0:1] = top
        out[1:2] = total
        out[2:3] = hits


def merge(a, b, ties=(), last=False):
    return pl.pallas_call(
        functools.partial(merge_kernel, last),
        out_shape=[arr((1, 2048), f32), arr((8, 128), f32)] if last else arr((3, 2048), f32),
        in_specs=[VM, VM] + [ANY] * len(ties),
        out_specs=[VM, VM] if last else VM,
        compiler_params=pltpu.CompilerParams(vmem_limit_bytes=4 * MIB),
        cost_estimate=cost(0, 2**16),
        name="merge",
    )(a, b, *ties)


def shards(queries, passages, positive):
    y, core, z, x = place()
    first = core == 0
    flat = passages.T
    got = swap(jnp.where(first, flat, queries))
    own = jnp.stack([jnp.where(first, queries, flat), got])
    down, up, far = hop(own, 3, False), hop(own, 1, False), hop(own, 2, False)
    across = hop(own, 0, True)
    down_across, up_across = hop(down, 0, True), hop(up, 0, True)
    far_across = hop(across, 2, False)
    chunks = [own, across, up, down, far, up_across, down_across, far_across]
    others = [swap(c) for c in chunks]

    aims = positive.reshape(4, 2, 2, 128)
    aims = jnp.where(x // 2 == 0, aims[:, 0], aims[:, 1]).transpose(1, 0, 2).reshape(1024)
    block = aims // 1024
    in_tile = (block // 4 == z) & ((block % 4 + 1) % 4 // 2 == (x + 1) % 4 // 2)
    aims = jnp.where(in_tile, block % 4 // 2 * 1024 + aims % 1024, -1)
    aims = jnp.broadcast_to(aims[:, None], (1024, 128))

    scores, keep, send = scores_of(chunks, others, aims)
    q_flip = flipped(chunks, others, keep)
    stats = merge(keep, swap(send))
    stats = merge(stats, hop(stats, 0, True), (q_flip,))
    stats = merge(stats, hop_xor(stats))
    own_lse, part = merge(stats, hop(stats, 2, False), last=True)
    got_lse, part = swap(own_lse), swap(part)

    outs = grads_of(
        1, ((1, 3), (2,), (0,)), chunks, others, (scores, aims, own_lse, got_lse, q_flip), [VM, VM, VM, VM, ANY], True, (part,)
    )
    keeps, recvs, slope = outs[:3], [swap(s) for s in outs[3:6]], outs[6]
    sides, beyond = join([keeps[0], recvs[0]]), join([keeps[1], recvs[1]])
    part = part + hop(part, 0, True)
    ties = (sides, beyond, part)
    sides, beyond = hop(sides, 0, True), hop(beyond, 2, False)
    across = [keeps[2], recvs[2]]
    outs = grads_of(0, ((1,), (3,), (2,), (0,)), chunks, others, (slope, q_flip), [ANY, ANY], False, ties)
    part = part + hop_xor(part)
    keeps, recvs = outs[:4], [swap(s) for s in outs[4:]]
    up = hop(join([keeps[0], recvs[0], sides], pick=0), 1, False)
    down = hop(join([keeps[1], recvs[1], sides], pick=1), 3, False)
    across = hop(join([*across, beyond]), 0, True)
    far = hop(join([keeps[2], recvs[2]], (part,)), 2, False)
    home = join([keeps[3], recvs[3]], (part,))
    part = part + hop(part, 2, False)
    mine, other = total([home, far, across, up, down], (part,))
    other = swap(other)
    grad_queries = jnp.where(first, mine, other)
    grad_passages = jnp.where(first, other, mine).T
    loss = (part + swap(part))[0, 0] / (32768.0 * log2_e)
    return loss, grad_queries, grad_passages


def solution(mesh):
    in_specs = (P(("row", "col"), None), P("col", "row"), P("row"))
    out_specs = (P(), P(("row", "col"), None), P("col", "row"))
    return jax.shard_map(shards, mesh=mesh, in_specs=in_specs, out_specs=out_specs, check_vma=False)
```

```python
import functools

import jax
import jax.numpy as jnp
from jax import lax
from jax.experimental import pallas as pl
from jax.experimental.pallas import tpu as pltpu
from jax.sharding import PartitionSpec as P

logit_scale = 40.0
log2_e = 1.4426950408889634
score_scale = logit_scale * log2_e
low = -1e30
AX = ("row", "col")
f32, bf16 = jnp.float32, jnp.bfloat16
MIB = 1024 * 1024


def lin(y, c, z, x):
    return ((y * 2 + c) * 4 + z) * 4 + x


def moves(step, turn):
    pairs = []
    for y in range(4):
        for z in range(4):
            for x in range(4):
                far_z, side = step(z, x, x ^ 1)
                pairs.append((lin(y, turn, z, x), lin(y, turn, far_z, side)))
                far_y, side = step(y, x, 3 - x)
                pairs.append((lin(y, 1 - turn, z, x), lin(far_y, 1 - turn, z, side)))
    return pairs


def hop(a, d, flip, turn=0):
    return lax.ppermute(a, AX, moves(lambda r, x, other: ((r + d) % 4, other if flip else x), turn))


def hop_xor(a, turn=0):
    return lax.ppermute(a, AX, moves(lambda r, x, other: (r ^ 1, x), turn))


def swap(a):
    return lax.ppermute(a, "row", [(i, i ^ 1) for i in range(8)])


def place():
    row, col = lax.axis_index("row"), lax.axis_index("col")
    return row // 2, row % 2, col // 4, col % 4


OFFSETS = [(0, 0), (2, 0), (3, 0), (1, 0), (0, 1), (3, 1), (1, 1), (2, 1)]


def load_copies(core, y, z, x, mine, theirs, q_dst, p_dst, sems):
    out = []
    for k, (d, flip) in enumerate(OFFSETS):
        slot = ((x % 2) ^ flip) * 4 + (z - d + 4) % 4
        far_y = (y - d + 4) % 4
        rank = (x // 2) ^ flip
        for which in range(2):
            copies = []
            q_src, p_src = (mine[k], theirs[k]) if which == 0 else (theirs[k], mine[k])
            if q_dst is not None:
                rows = pl.ds(pl.multiple_of(slot * 128, 128), 128)
                copies.append(pltpu.make_async_copy(q_src.at[which], q_dst.at[rows], sems.at[k, 0]))
            if p_dst is not None:
                for part in range(2):
                    rows = pl.ds(pl.multiple_of(far_y * 256 + (1 - part) * 128, 128), 128)
                    copies.append(
                        pltpu.make_async_copy(p_src.at[part], p_dst.at[rank, rows], sems.at[k, 1 + part])
                    )
            out.append((which, copies))
    return out


def run_copies(core, groups, start):
    for which in range(2):

        @pl.when(core == which)
        def _():
            for w, copies in groups:
                if w == which:
                    for copy in copies:
                        copy.start() if start else copy.wait()


TILE = 32


def lane_groups():
    return [(g // 8, slice(g % 8 * 128, g % 8 * 128 + 128)) for g in range(16)]


def fold(a):
    return sum(a[r : r + 8] for r in range(0, a.shape[0], 8))


def score_kernel(*refs):
    mine, theirs, (aims, sv, keep, send, qv, pt, target, row_top, row_sum, col_top, sems) = (
        refs[:8],
        refs[8:16],
        refs[16:],
    )
    y, core, z, x = place()
    groups = load_copies(core, y, z, x, mine, theirs, qv, pt, sems)
    run_copies(core, groups, True)
    for s in range(8):
        rows = slice(s * 128, s * 128 + 128)
        target[rows, :] = jnp.broadcast_to(aims[:, rows], (128, 128)).T
    run_copies(core, groups, False)
    for h in range(2):
        for n in range(2):
            cols = slice(n * 512, n * 512 + 512)
            s = score_scale * jnp.dot(qv[...], pt[h, :, cols], preferred_element_type=f32)
            sv[h, :, cols] = s
            col_top[h, :, cols] = jnp.broadcast_to(jnp.max(s, axis=0, keepdims=True), (8, 512))
            top = jnp.maximum(
                jnp.maximum(s[:, :128], s[:, 128:256]), jnp.maximum(s[:, 256:384], s[:, 384:])
            )
            row_top[...] = top if h == n == 0 else jnp.maximum(row_top[...], top)
    tops = []
    for s in range(8):
        rows = slice(s * 128, s * 128 + 128)
        top = jnp.max(row_top[rows, :].T, axis=0, keepdims=True)
        tops.append(top)
        row_top[rows, :] = jnp.broadcast_to(top, (128, 128)).T
    lanes = lax.broadcasted_iota(jnp.int32, (TILE, 128), 1).astype(f32)

    def step(i, carry):
        col_acc, hits = carry
        rows = pl.ds(pl.multiple_of(i * TILE, TILE), TILE)
        top, aim = row_top[rows, :], target[rows, :]
        total, cols = jnp.zeros((TILE, 128), f32), []
        for g, (h, at) in enumerate(lane_groups()):
            t = sv[h, rows, at]
            total = total + jnp.exp2(t - top)
            cols.append(col_acc[g] + fold(jnp.exp2(t - col_top[h, 0:1, at])))
            hits = hits + fold(jnp.where(lanes == aim - g * 128, t, 0.0))
        row_sum[rows, :] = total
        return tuple(cols), hits

    zero = jnp.zeros((8, 128), f32)
    col_acc, hits = lax.fori_loop(0, 1024 // TILE, step, ((zero,) * 16, zero))
    hits = jnp.sum(hits, axis=0, keepdims=True)

    def fill(rows_ref, cols_ref, first):
        off = 0 if first else 1024
        for s in range(8):
            at = slice(off + s * 128, off + s * 128 + 128)
            rows_ref[0:1, at] = tops[s]
            rows_ref[1:2, at] = jnp.sum(row_sum[s * 128 : s * 128 + 128, :].T, axis=0, keepdims=True)
        gap = slice(1024 - off, 2048 - off)
        rows_ref[0:1, gap] = jnp.full((1, 1024), low, f32)
        rows_ref[1:2, gap] = jnp.zeros((1, 1024), f32)
        rows_ref[2:3, :] = jnp.zeros((1, 2048), f32)
        rows_ref[2:3, :128] = hits
        for h in range(2):
            cols_ref[0:1, h * 1024 : h * 1024 + 1024] = col_top[h, 0:1, :]
        for g in range(16):
            cols_ref[1:2, g * 128 : g * 128 + 128] = jnp.sum(col_acc[g], axis=0, keepdims=True)
        cols_ref[2:3, :] = jnp.zeros((1, 2048), f32)

    @pl.when(core == 0)
    def _():
        fill(keep, send, True)

    @pl.when(core == 1)
    def _():
        fill(send, keep, False)


def slope_kernel(sv, target, own_lse, got_lse, part, slope, part_out, row_lse):
    part_out[...] = part[...]
    first = place()[1] == 0
    mine_lse, their_lse = own_lse[...], got_lse[...]
    rows_lse = jnp.where(first, mine_lse[:, :1024], their_lse[:, 1024:])
    cols_lse = jnp.where(first, their_lse, mine_lse)
    for s in range(8):
        row_lse[s * 128 : s * 128 + 128, :] = jnp.broadcast_to(
            rows_lse[:, s * 128 : s * 128 + 128], (128, 128)
        ).T
    lanes = lax.broadcasted_iota(jnp.int32, (TILE, 128), 1).astype(f32)

    def step(i, carry):
        rows = pl.ds(pl.multiple_of(i * TILE, TILE), TILE)
        aim, lse = target[rows, :], row_lse[rows, :]
        for g, (h, at) in enumerate(lane_groups()):
            t = sv[h, rows, at]
            e = 0.5 * (jnp.exp2(t - lse) + jnp.exp2(t - cols_lse[:, g * 128 : g * 128 + 128]))
            slope[h, rows, at] = jnp.where(lanes == aim - g * 128, e - 1.0, e).astype(bf16)
        return carry

    lax.fori_loop(0, 1024 // TILE, step, 0)


def grad_kernel(flip, order, n_ties, *refs):
    n = len(order)
    steps = [(g, i, d) for g, group in enumerate(order) for i, d in enumerate(group)]
    (slope, qt, pt, part), refs = refs[:4], refs[4 + n_ties :]
    keeps, sends, (part_out, gq, gp, zeros, out_sems) = refs[:n], refs[n : 2 * n], refs[2 * n :]
    part_out[...] = part[...]
    y, core, z, x = place()
    zeros[...] = jnp.zeros(zeros.shape, bf16)
    half = (x % 2) ^ flip
    rank = (x // 2) ^ flip
    rows = pl.ds(pl.multiple_of(half * 512, 512), 512)

    def send_queries(which):
        copies = []
        for k, (g, i, d) in enumerate(steps):
            to = (sends if which else keeps)[g].at[i]
            at = pl.ds(pl.multiple_of((z + d) % 4 * 128, 128), 128)
            copies.append(pltpu.make_async_copy(gq.at[at], to.at[which], out_sems.at[k, 0]))
            copies.append(pltpu.make_async_copy(zeros, to.at[1 - which], out_sems.at[k, 1]))
        return copies

    def send_passages(which, m, cut):
        copies = []
        for k, (g, i, d) in enumerate(steps):
            to = (keeps if which else sends)[g].at[i]
            for part in range(2):
                at = pl.ds(pl.multiple_of((y + d) % 4 * 256 + (1 - part) * 128, 128), 128)
                copies.append(
                    pltpu.make_async_copy(gp.at[at, cut], to.at[part, :, cut], out_sems.at[k, 2 + 2 * m + part])
                )
        return copies

    def start(make):
        for which in range(2):

            @pl.when(core == which)
            def _():
                for copy in make(which):
                    copy.start()

    for m in range(4):
        cut = slice(m * 256, m * 256 + 256)
        g = sum(
            lax.dot_general(
                slope[h, rows, :], pt[h, cut, :], (((1,), (1,)), ((), ())), preferred_element_type=f32
            )
            for h in range(2)
        )
        gq[:, cut] = (logit_scale * g).astype(bf16)
    start(send_queries)
    cuts = [slice(m * 512, m * 512 + 512) for m in range(2)]
    for m, cut in enumerate(cuts):
        g = jnp.dot(qt[...], slope[rank, :, cut], preferred_element_type=f32)
        gp[:, cut] = (logit_scale * g).astype(bf16)
        start(functools.partial(send_passages, m=m, cut=cut))

    for which in range(2):

        @pl.when(core == which)
        def _():
            for copy in send_queries(which) + [c for m, cut in enumerate(cuts) for c in send_passages(which, m, cut)]:
                copy.wait()


ANY = pl.BlockSpec(memory_space=pl.ANY)
VM = pl.BlockSpec(memory_space=pltpu.VMEM)


def arr(shape, dtype):
    return jax.ShapeDtypeStruct(shape, dtype)


def cost(flops, nbytes):
    return pl.CostEstimate(flops=flops, bytes_accessed=nbytes, transcendentals=0)


def scores_of(mine, theirs, aims):
    return pl.pallas_call(
        score_kernel,
        out_shape=(
            arr((2, 1024, 1024), f32),
            arr((3, 2048), f32),
            arr((3, 2048), f32),
            arr((1024, 1024), bf16),
            arr((2, 1024, 1024), bf16),
            arr((1024, 128), f32),
        ),
        in_specs=[ANY] * 16 + [VM],
        out_specs=(VM,) * 6,
        scratch_shapes=[
            pltpu.VMEM((1024, 128), f32),
            pltpu.VMEM((1024, 128), f32),
            pltpu.VMEM((2, 8, 1024), f32),
            pltpu.SemaphoreType.DMA((8, 3)),
        ],
        compiler_params=pltpu.CompilerParams(vmem_limit_bytes=12 * MIB),
        cost_estimate=cost(2 * 1024**2 * 2048, 16 * MIB),
        name="scores",
    )(*mine, *theirs, aims)


def flip_kernel(q, out):
    for m in range(8):
        out[:, m * 128 : m * 128 + 128] = q[m * 128 : m * 128 + 128, :].T


def flipped(q):
    return pl.pallas_call(
        flip_kernel,
        out_shape=arr(q.shape, bf16),
        in_specs=[VM],
        out_specs=VM,
        compiler_params=pltpu.CompilerParams(vmem_limit_bytes=8 * MIB),
        cost_estimate=cost(0, 4 * MIB),
        name="flip",
    )(q)


def entry_kernel(q, p, mine, send):
    first = place()[1] == 0
    flat = p[...].T
    mine[...] = jnp.where(first, q[...], flat)
    send[...] = jnp.where(first, flat, q[...])


def entry(q, p):
    return pl.pallas_call(
        entry_kernel,
        out_shape=[arr((128, 1024), bf16)] * 2,
        in_specs=[VM] * 2,
        out_specs=[VM] * 2,
        compiler_params=pltpu.CompilerParams(vmem_limit_bytes=8 * MIB),
        cost_estimate=cost(0, MIB),
        name="entry",
    )(q, p)


def finish_kernel(mine, other, grad_queries, grad_passages):
    first = place()[1] == 0
    a, b = mine[...], other[...]
    grad_queries[...] = jnp.where(first, a, b)
    grad_passages[...] = jnp.where(first, b, a).T


def finish(mine, other):
    return pl.pallas_call(
        finish_kernel,
        out_shape=[arr((128, 1024), f32), arr((1024, 128), f32)],
        in_specs=[VM] * 2,
        out_specs=[VM] * 2,
        compiler_params=pltpu.CompilerParams(vmem_limit_bytes=8 * MIB),
        cost_estimate=cost(0, 2 * MIB),
        name="finish",
    )(mine, other)


def slope_of(scores, target, own_lse, got_lse, part):
    return pl.pallas_call(
        slope_kernel,
        out_shape=[arr((2, 1024, 1024), bf16), arr((8, 128), f32)],
        in_specs=[VM] * 5,
        out_specs=[VM] * 2,
        scratch_shapes=[pltpu.VMEM((1024, 128), f32)],
        compiler_params=pltpu.CompilerParams(vmem_limit_bytes=8 * MIB),
        cost_estimate=cost(2 * 1024**2 * 2048, 12 * MIB),
        name="slope",
    )(scores, target, own_lse, got_lse, part)


def grads_of(flip, order, operands, ties):
    chunks = [arr((len(group), 2, 128, 1024), bf16) for group in order]
    return pl.pallas_call(
        functools.partial(grad_kernel, flip, order, len(ties)),
        out_shape=chunks * 2 + [arr((8, 128), f32)],
        in_specs=[VM] * len(operands) + [ANY] * len(ties),
        out_specs=[VM] * (2 * len(chunks) + 1),
        scratch_shapes=[
            pltpu.VMEM((512, 1024), bf16),
            pltpu.VMEM((1024, 1024), bf16),
            pltpu.VMEM((128, 1024), bf16),
            pltpu.SemaphoreType.DMA((4, 6)),
        ],
        compiler_params=pltpu.CompilerParams(vmem_limit_bytes=12 * MIB),
        cost_estimate=cost(2 * 1024**2 * 2048, 20 * MIB),
        name="grads_far" if flip else "grads_near",
    )(*operands, *ties)


def join_kernel(picks, *refs):
    out = refs[-1]
    parts = [r[...] if p is None else r[p : p + 1] for p, r in zip(picks, refs)]
    out[...] = sum(p.astype(f32) for p in parts).astype(bf16)


def join(terms, ties=(), pick=None):
    a, n = terms[0], len(terms)
    return pl.pallas_call(
        functools.partial(join_kernel, [None] * (n - 1) + [pick]),
        out_shape=arr(a.shape, bf16),
        in_specs=[VM] * n + [ANY] * len(ties),
        out_specs=VM,
        compiler_params=pltpu.CompilerParams(vmem_limit_bytes=8 * MIB),
        cost_estimate=cost(a.size, 6 * a.size),
        name="join",
    )(*terms, *ties)


def total_kernel(n, *refs):
    mine, other = refs[-2:]
    mine[...] = sum(r[0, 0].astype(f32) for r in refs[:n])
    other[...] = sum(r[0, 1].astype(f32) for r in refs[:n])


def total(terms, ties=()):
    return pl.pallas_call(
        functools.partial(total_kernel, len(terms)),
        out_shape=[arr((128, 1024), f32)] * 2,
        in_specs=[VM] * len(terms) + [ANY] * len(ties),
        out_specs=[VM] * 2,
        compiler_params=pltpu.CompilerParams(vmem_limit_bytes=8 * MIB),
        cost_estimate=cost(5 * 2**18, 4 * MIB),
        name="total",
    )(*terms, *ties)


def merge_kernel(last, a, b, *refs):
    top = jnp.maximum(a[0:1], b[0:1])
    total = a[1:2] * jnp.exp2(a[0:1] - top) + b[1:2] * jnp.exp2(b[0:1] - top)
    hits = a[2:3] + b[2:3]
    if last:
        lse, part = refs[-2:]
        lse[...] = top + jnp.log2(total)
        figure = jnp.sum(lse[...] - 2.0 * hits, axis=1, keepdims=True)
        part[...] = jnp.broadcast_to(figure, (8, 128))
    else:
        out = refs[-1]
        out[0:1] = top
        out[1:2] = total
        out[2:3] = hits


def merge(a, b, ties=(), last=False):
    return pl.pallas_call(
        functools.partial(merge_kernel, last),
        out_shape=[arr((1, 2048), f32), arr((8, 128), f32)] if last else arr((3, 2048), f32),
        in_specs=[VM, VM] + [ANY] * len(ties),
        out_specs=[VM, VM] if last else VM,
        compiler_params=pltpu.CompilerParams(vmem_limit_bytes=4 * MIB),
        cost_estimate=cost(0, 2**16),
        name="merge",
    )(a, b, *ties)


def shards(queries, passages, positive):
    y, core, z, x = place()
    mine, send = entry(queries, passages)
    own = jnp.stack([mine, swap(send)])
    down, up, far = hop(own, 3, False), hop(own, 1, False), hop(own, 2, False)
    across = hop(own, 0, True)
    down_across, up_across = hop(down, 0, True), hop(up, 0, True)
    far_across = hop(across, 2, False)
    chunks = [own, far, down, up, across, down_across, up_across, far_across]
    others = [swap(c) for c in chunks]

    aims = positive.reshape(4, 2, 2, 128)
    aims = jnp.where(x // 2 == 0, aims[:, 0], aims[:, 1]).transpose(1, 0, 2).reshape(1024)
    block = aims // 1024
    in_tile = (block // 4 == z) & ((block % 4 + 1) % 4 // 2 == (x + 1) % 4 // 2)
    aims = jnp.where(in_tile, block % 4 // 2 * 1024 + aims % 1024, -1)
    aims = aims.astype(f32).reshape(1, 1024)

    scores, keep, send, q_tile, p_tile, target = scores_of(chunks, others, aims)
    q_flip = flipped(q_tile)
    stats = merge(keep, swap(send))
    stats = merge(stats, hop(stats, 0, True), (q_flip,))
    stats = merge(stats, hop_xor(stats))
    own_lse, part = merge(stats, hop(stats, 2, False), last=True)
    slope, part = slope_of(scores, target, own_lse, swap(own_lse), part)

    outs = grads_of(1, ((1, 3), (2,), (0,)), (slope, q_flip, p_tile, part), ())
    part = part + hop_xor(part, 1)
    keeps, recvs = outs[:3], [swap(s) for s in outs[3:6]]
    sides, beyond = join([keeps[0], recvs[0]], (part,)), join([keeps[1], recvs[1]])
    part = part + hop(part, 2, False, 1)
    ties = (sides, beyond)
    sides, beyond = hop(sides, 0, True), hop(beyond, 2, False)
    across = [keeps[2], recvs[2]]
    outs = grads_of(0, ((1,), (3,), (2,), (0,)), (slope, q_flip, p_tile, part), ties)
    part = outs[8] + hop(outs[8], 0, True, 1)
    keeps, recvs = outs[:4], [swap(s) for s in outs[4:8]]
    up = hop(join([keeps[0], recvs[0], sides], pick=0), 1, False)
    down = hop(join([keeps[1], recvs[1], sides], pick=1), 3, False)
    across = hop(join([*across, beyond]), 0, True)
    far = hop(join([keeps[2], recvs[2]]), 2, False)
    home = join([keeps[3], recvs[3]], (part,))
    part = part + swap(part)
    mine, other = total([home, far, across, up, down], (part,))
    grad_queries, grad_passages = finish(mine, swap(other))
    loss = part[0, 0] / (32768.0 * log2_e)
    return loss, grad_queries, grad_passages


def solution(mesh):
    in_specs = (P(("row", "col"), None), P("col", "row"), P("row"))
    out_specs = (P(), P(("row", "col"), None), P("col", "row"))
    return jax.shard_map(shards, mesh=mesh, in_specs=in_specs, out_specs=out_specs, check_vma=False)
```

```python
import functools

import jax
import jax.numpy as jnp
from jax import lax
from jax.experimental import pallas as pl
from jax.experimental.pallas import tpu as pltpu
from jax.sharding import PartitionSpec as P

logit_scale = 40.0
log2_e = 1.4426950408889634
score_scale = logit_scale * log2_e
low = -1e30
AX = ("row", "col")
f32, bf16 = jnp.float32, jnp.bfloat16
MIB = 1024 * 1024


def lin(y, c, z, x):
    return ((y * 2 + c) * 4 + z) * 4 + x


def moves(step, turn):
    pairs = []
    for y in range(4):
        for z in range(4):
            for x in range(4):
                far_z, side = step(z, x, x ^ 1)
                pairs.append((lin(y, turn, z, x), lin(y, turn, far_z, side)))
                far_y, side = step(y, x, 3 - x)
                pairs.append((lin(y, 1 - turn, z, x), lin(far_y, 1 - turn, z, side)))
    return pairs


def hop(a, d, flip, turn=0):
    return lax.ppermute(a, AX, moves(lambda r, x, other: ((r + d) % 4, other if flip else x), turn))


def hop_xor(a, turn=0):
    return lax.ppermute(a, AX, moves(lambda r, x, other: (r ^ 1, x), turn))


def swap(a):
    return lax.ppermute(a, "row", [(i, i ^ 1) for i in range(8)])


def place():
    row, col = lax.axis_index("row"), lax.axis_index("col")
    return row // 2, row % 2, col // 4, col % 4


OFFSETS = [(2, 0), (1, 0), (0, 1), (3, 1), (0, 0), (3, 0), (1, 1), (2, 1)]


def load_copies(core, y, z, x, mine, theirs, q_dst, p_dst, sems):
    out = []
    for k, (d, flip) in enumerate(OFFSETS):
        slot = ((x % 2) ^ flip) * 4 + (z - d + 4) % 4
        far_y = (y - d + 4) % 4
        rank = (x // 2) ^ flip
        for which in range(2):
            copies = []
            q_src, p_src = (mine[k], theirs[k]) if which == 0 else (theirs[k], mine[k])
            if q_dst is not None:
                rows = pl.ds(pl.multiple_of(slot * 128, 128), 128)
                copies.append(pltpu.make_async_copy(q_src.at[which], q_dst.at[rows], sems.at[k, 0]))
            if p_dst is not None:
                for part in range(2):
                    rows = pl.ds(pl.multiple_of(far_y * 256 + (1 - part) * 128, 128), 128)
                    copies.append(
                        pltpu.make_async_copy(p_src.at[part], p_dst.at[rank, rows], sems.at[k, 1 + part])
                    )
            out.append((which, copies))
    return out


def run_copies(core, groups, start):
    for which in range(2):

        @pl.when(core == which)
        def _():
            for w, copies in groups:
                if w == which:
                    for copy in copies:
                        copy.start() if start else copy.wait()


TILE = 32


def lane_groups():
    return [(g // 8, slice(g % 8 * 128, g % 8 * 128 + 128)) for g in range(16)]


def fold(a):
    return sum(a[r : r + 8] for r in range(0, a.shape[0], 8))


def score_kernel(*refs):
    mine, theirs, (target, sv, keep, send, qv, pt, row_top, row_sum, col_top, sems) = (
        refs[:8],
        refs[8:16],
        refs[16:],
    )
    y, core, z, x = place()
    groups = load_copies(core, y, z, x, mine, theirs, qv, pt, sems)
    run_copies(core, groups, True)
    run_copies(core, groups, False)
    for h in range(2):
        for n in range(2):
            cols = slice(n * 512, n * 512 + 512)
            s = score_scale * jnp.dot(qv[...], pt[h, :, cols], preferred_element_type=f32)
            sv[h, :, cols] = s
            col_top[h, :, cols] = jnp.broadcast_to(jnp.max(s, axis=0, keepdims=True), (8, 512))
            top = jnp.maximum(
                jnp.maximum(s[:, :128], s[:, 128:256]), jnp.maximum(s[:, 256:384], s[:, 384:])
            )
            row_top[...] = top if h == n == 0 else jnp.maximum(row_top[...], top)
    tops = []
    for s in range(8):
        rows = slice(s * 128, s * 128 + 128)
        top = jnp.max(row_top[rows, :].T, axis=0, keepdims=True)
        tops.append(top)
        row_top[rows, :] = jnp.broadcast_to(top, (128, 128)).T
    lanes = lax.broadcasted_iota(jnp.int32, (TILE, 128), 1).astype(f32)

    def step(i, carry):
        col_acc, hits = carry
        rows = pl.ds(pl.multiple_of(i * TILE, TILE), TILE)
        top, aim = row_top[rows, :], target[rows, :]
        total, cols = jnp.zeros((TILE, 128), f32), []
        for g, (h, at) in enumerate(lane_groups()):
            t = sv[h, rows, at]
            total = total + jnp.exp2(t - top)
            cols.append(col_acc[g] + fold(jnp.exp2(t - col_top[h, 0:1, at])))
            hits = hits + fold(jnp.where(lanes == aim - g * 128, t, 0.0))
        row_sum[rows, :] = total
        return tuple(cols), hits

    zero = jnp.zeros((8, 128), f32)
    col_acc, hits = lax.fori_loop(0, 1024 // TILE, step, ((zero,) * 16, zero))
    hits = jnp.sum(hits, axis=0, keepdims=True)

    def fill(rows_ref, cols_ref, first):
        off = 0 if first else 1024
        for s in range(8):
            at = slice(off + s * 128, off + s * 128 + 128)
            rows_ref[0:1, at] = tops[s]
            rows_ref[1:2, at] = jnp.sum(row_sum[s * 128 : s * 128 + 128, :].T, axis=0, keepdims=True)
        gap = slice(1024 - off, 2048 - off)
        rows_ref[0:1, gap] = jnp.full((1, 1024), low, f32)
        rows_ref[1:2, gap] = jnp.zeros((1, 1024), f32)
        rows_ref[2:3, :] = jnp.zeros((1, 2048), f32)
        rows_ref[2:3, :128] = hits
        for h in range(2):
            cols_ref[0:1, h * 1024 : h * 1024 + 1024] = col_top[h, 0:1, :]
        for g in range(16):
            cols_ref[1:2, g * 128 : g * 128 + 128] = jnp.sum(col_acc[g], axis=0, keepdims=True)
        cols_ref[2:3, :] = jnp.zeros((1, 2048), f32)

    @pl.when(core == 0)
    def _():
        fill(keep, send, True)

    @pl.when(core == 1)
    def _():
        fill(send, keep, False)


def slope_kernel(sv, target, own_lse, got_lse, part, slope, part_out, row_lse):
    part_out[...] = part[...]
    first = place()[1] == 0
    mine_lse, their_lse = own_lse[...], got_lse[...]
    rows_lse = jnp.where(first, mine_lse[:, :1024], their_lse[:, 1024:])
    cols_lse = jnp.where(first, their_lse, mine_lse)
    for s in range(8):
        row_lse[s * 128 : s * 128 + 128, :] = jnp.broadcast_to(
            rows_lse[:, s * 128 : s * 128 + 128], (128, 128)
        ).T
    lanes = lax.broadcasted_iota(jnp.int32, (TILE, 128), 1).astype(f32)

    def step(i, carry):
        rows = pl.ds(pl.multiple_of(i * TILE, TILE), TILE)
        aim, lse = target[rows, :], row_lse[rows, :]
        for g, (h, at) in enumerate(lane_groups()):
            t = sv[h, rows, at]
            e = 0.5 * (jnp.exp2(t - lse) + jnp.exp2(t - cols_lse[:, g * 128 : g * 128 + 128]))
            slope[h, rows, at] = jnp.where(lanes == aim - g * 128, e - 1.0, e).astype(bf16)
        return carry

    lax.fori_loop(0, 1024 // TILE, step, 0)


def grad_kernel(flip, order, n_ties, *refs):
    n = len(order)
    steps = [(g, i, d) for g, group in enumerate(order) for i, d in enumerate(group)]
    (slope, qt, pt, part), refs = refs[:4], refs[4 + n_ties :]
    keeps, sends, (part_out, gq, gp, zeros, out_sems) = refs[:n], refs[n : 2 * n], refs[2 * n :]
    part_out[...] = part[...]
    y, core, z, x = place()
    zeros[...] = jnp.zeros(zeros.shape, bf16)
    half = (x % 2) ^ flip
    rank = (x // 2) ^ flip
    rows = pl.ds(pl.multiple_of(half * 512, 512), 512)

    def send_queries(which):
        copies = []
        for k, (g, i, d) in enumerate(steps):
            to = (sends if which else keeps)[g].at[i]
            at = pl.ds(pl.multiple_of((z + d) % 4 * 128, 128), 128)
            copies.append(pltpu.make_async_copy(gq.at[at], to.at[which], out_sems.at[k, 0]))
            copies.append(pltpu.make_async_copy(zeros, to.at[1 - which], out_sems.at[k, 1]))
        return copies

    def send_passages(which, m, cut):
        copies = []
        for k, (g, i, d) in enumerate(steps):
            to = (keeps if which else sends)[g].at[i]
            for part in range(2):
                at = pl.ds(pl.multiple_of((y + d) % 4 * 256 + (1 - part) * 128, 128), 128)
                copies.append(
                    pltpu.make_async_copy(gp.at[at, cut], to.at[part, :, cut], out_sems.at[k, 2 + 2 * m + part])
                )
        return copies

    def start(make):
        for which in range(2):

            @pl.when(core == which)
            def _():
                for copy in make(which):
                    copy.start()

    for m in range(4):
        cut = slice(m * 256, m * 256 + 256)
        g = sum(
            lax.dot_general(
                slope[h, rows, :], pt[h, cut, :], (((1,), (1,)), ((), ())), preferred_element_type=f32
            )
            for h in range(2)
        )
        gq[:, cut] = (logit_scale * g).astype(bf16)
    start(send_queries)
    cuts = [slice(m * 512, m * 512 + 512) for m in range(2)]
    for m, cut in enumerate(cuts):
        g = jnp.dot(qt[...], slope[rank, :, cut], preferred_element_type=f32)
        gp[:, cut] = (logit_scale * g).astype(bf16)
        start(functools.partial(send_passages, m=m, cut=cut))

    for which in range(2):

        @pl.when(core == which)
        def _():
            for copy in send_queries(which) + [c for m, cut in enumerate(cuts) for c in send_passages(which, m, cut)]:
                copy.wait()


ANY = pl.BlockSpec(memory_space=pl.ANY)
VM = pl.BlockSpec(memory_space=pltpu.VMEM)


def arr(shape, dtype):
    return jax.ShapeDtypeStruct(shape, dtype)


def cost(flops, nbytes):
    return pl.CostEstimate(flops=flops, bytes_accessed=nbytes, transcendentals=0)


def scores_of(mine, theirs, target):
    return pl.pallas_call(
        score_kernel,
        out_shape=(
            arr((2, 1024, 1024), f32),
            arr((3, 2048), f32),
            arr((3, 2048), f32),
            arr((1024, 1024), bf16),
            arr((2, 1024, 1024), bf16),
        ),
        in_specs=[ANY] * 16 + [VM],
        out_specs=(VM,) * 5,
        scratch_shapes=[
            pltpu.VMEM((1024, 128), f32),
            pltpu.VMEM((1024, 128), f32),
            pltpu.VMEM((2, 8, 1024), f32),
            pltpu.SemaphoreType.DMA((8, 3)),
        ],
        compiler_params=pltpu.CompilerParams(vmem_limit_bytes=18 * MIB),
        cost_estimate=cost(2 * 1024**2 * 2048, 16 * MIB),
        name="scores",
    )(*mine, *theirs, target)


def flip_kernel(q, out):
    for m in range(8):
        out[:, m * 128 : m * 128 + 128] = q[m * 128 : m * 128 + 128, :].T


def flipped(q):
    return pl.pallas_call(
        flip_kernel,
        out_shape=arr(q.shape, bf16),
        in_specs=[VM],
        out_specs=VM,
        compiler_params=pltpu.CompilerParams(vmem_limit_bytes=8 * MIB),
        cost_estimate=cost(0, 4 * MIB),
        name="flip",
    )(q)


def entry_kernel(q_in, p_in, mine, send, q, p, sems):
    copies = [pltpu.make_async_copy(q_in, q, sems.at[0]), pltpu.make_async_copy(p_in, p, sems.at[1])]
    for copy in copies:
        copy.start()
    for copy in copies:
        copy.wait()
    first = place()[1] == 0
    flat = p[...].T
    mine[...] = jnp.where(first, q[...], flat)
    send[...] = jnp.where(first, flat, q[...])


def entry(q, p):
    return pl.pallas_call(
        entry_kernel,
        out_shape=[arr((128, 1024), bf16)] * 2,
        in_specs=[ANY] * 2,
        out_specs=[VM] * 2,
        scratch_shapes=[pltpu.VMEM(q.shape, bf16), pltpu.VMEM(p.shape, bf16), pltpu.SemaphoreType.DMA((2,))],
        compiler_params=pltpu.CompilerParams(vmem_limit_bytes=4 * MIB),
        cost_estimate=cost(0, MIB),
        name="entry",
    )(q, p)


def aim_kernel(positive, out):
    _, _, z, x = place()
    side = (x + 1) % 4 // 2
    for s in range(8):
        p = positive[pl.ds(s % 4 * 4 + x // 2 * 2 + s // 4, 1), :]
        far_z, far_x = p >> 12, (p >> 10) & 3
        inside = (far_z == z) & ((((far_x + 1) & 3) >> 1) == side)
        aim = jnp.where(inside, (far_x >> 1) * 1024 + (p & 1023), -1).astype(f32)
        out[s * 128 : s * 128 + 128, :] = jnp.broadcast_to(aim, (128, 128)).T


def aims_of(positive):
    return pl.pallas_call(
        aim_kernel,
        out_shape=arr((1024, 128), f32),
        in_specs=[VM],
        out_specs=VM,
        compiler_params=pltpu.CompilerParams(vmem_limit_bytes=4 * MIB),
        cost_estimate=cost(0, MIB),
        name="aims",
    )(positive.reshape(16, 128))


def after_kernel(a, *refs):
    refs[-1][...] = a[...]


def after(a, *ties):
    return pl.pallas_call(
        after_kernel,
        out_shape=arr(a.shape, a.dtype),
        in_specs=[VM] + [ANY] * len(ties),
        out_specs=VM,
        compiler_params=pltpu.CompilerParams(vmem_limit_bytes=4 * MIB),
        cost_estimate=cost(0, 1024),
        name="after",
    )(a, *ties)


def finish_kernel(mine, other, grad_queries, grad_passages):
    first = place()[1] == 0
    a, b = mine[...], other[...]
    grad_queries[...] = jnp.where(first, a, b)
    grad_passages[...] = jnp.where(first, b, a).T


def finish(mine, other):
    return pl.pallas_call(
        finish_kernel,
        out_shape=[arr((128, 1024), f32), arr((1024, 128), f32)],
        in_specs=[VM] * 2,
        out_specs=[VM] * 2,
        compiler_params=pltpu.CompilerParams(vmem_limit_bytes=8 * MIB),
        cost_estimate=cost(0, 2 * MIB),
        name="finish",
    )(mine, other)


def slope_of(scores, target, own_lse, got_lse, part):
    return pl.pallas_call(
        slope_kernel,
        out_shape=[arr((2, 1024, 1024), bf16), arr((8, 128), f32)],
        in_specs=[VM] * 5,
        out_specs=[VM] * 2,
        scratch_shapes=[pltpu.VMEM((1024, 128), f32)],
        compiler_params=pltpu.CompilerParams(vmem_limit_bytes=8 * MIB),
        cost_estimate=cost(2 * 1024**2 * 2048, 12 * MIB),
        name="slope",
    )(scores, target, own_lse, got_lse, part)


def grads_of(flip, order, operands, ties):
    chunks = [arr((len(group), 2, 128, 1024), bf16) for group in order]
    return pl.pallas_call(
        functools.partial(grad_kernel, flip, order, len(ties)),
        out_shape=chunks * 2 + [arr((8, 128), f32)],
        in_specs=[VM] * len(operands) + [ANY] * len(ties),
        out_specs=[VM] * (2 * len(chunks) + 1),
        scratch_shapes=[
            pltpu.VMEM((512, 1024), bf16),
            pltpu.VMEM((1024, 1024), bf16),
            pltpu.VMEM((128, 1024), bf16),
            pltpu.SemaphoreType.DMA((4, 6)),
        ],
        compiler_params=pltpu.CompilerParams(vmem_limit_bytes=12 * MIB),
        cost_estimate=cost(2 * 1024**2 * 2048, 20 * MIB),
        name="grads_far" if flip else "grads_near",
    )(*operands, *ties)


def join_kernel(picks, *refs):
    out = refs[-1]
    parts = [r[...] if p is None else r[p : p + 1] for p, r in zip(picks, refs)]
    out[...] = sum(p.astype(f32) for p in parts).astype(bf16)


def join(terms, ties=(), pick=None):
    a, n = terms[0], len(terms)
    return pl.pallas_call(
        functools.partial(join_kernel, [None] * (n - 1) + [pick]),
        out_shape=arr(a.shape, bf16),
        in_specs=[VM] * n + [ANY] * len(ties),
        out_specs=VM,
        compiler_params=pltpu.CompilerParams(vmem_limit_bytes=8 * MIB),
        cost_estimate=cost(a.size, 6 * a.size),
        name="join",
    )(*terms, *ties)


def total_kernel(n, *refs):
    mine, other = refs[-2:]
    mine[...] = sum(r[0, 0].astype(f32) for r in refs[:n])
    other[...] = sum(r[0, 1].astype(f32) for r in refs[:n])


def total(terms, ties=()):
    return pl.pallas_call(
        functools.partial(total_kernel, len(terms)),
        out_shape=[arr((128, 1024), f32)] * 2,
        in_specs=[VM] * len(terms) + [ANY] * len(ties),
        out_specs=[VM] * 2,
        compiler_params=pltpu.CompilerParams(vmem_limit_bytes=8 * MIB),
        cost_estimate=cost(5 * 2**18, 4 * MIB),
        name="total",
    )(*terms, *ties)


def merge_kernel(n, last, *refs):
    ins = refs[:n]
    top = ins[0][0:1]
    for a in ins[1:]:
        top = jnp.maximum(top, a[0:1])
    total = sum(a[1:2] * jnp.exp2(a[0:1] - top) for a in ins)
    hits = sum(a[2:3] for a in ins)
    if last:
        lse, part = refs[-2:]
        lse[...] = top + jnp.log2(total)
        figure = jnp.sum(lse[...] - 2.0 * hits, axis=1, keepdims=True)
        part[...] = jnp.broadcast_to(figure, (8, 128))
    else:
        out = refs[-1]
        out[0:1] = top
        out[1:2] = total
        out[2:3] = hits


def merge(ins, ties=(), last=False):
    return pl.pallas_call(
        functools.partial(merge_kernel, len(ins), last),
        out_shape=[arr((1, 2048), f32), arr((8, 128), f32)] if last else arr((3, 2048), f32),
        in_specs=[VM] * len(ins) + [ANY] * len(ties),
        out_specs=[VM, VM] if last else VM,
        compiler_params=pltpu.CompilerParams(vmem_limit_bytes=4 * MIB),
        cost_estimate=cost(0, 2**16),
        name="merge",
    )(*ins, *ties)


def shards(queries, passages, positive):
    mine, send = entry(queries, passages)
    own = jnp.stack([mine, swap(send)])
    down, up, far = hop(own, 3, False), hop(own, 1, False), hop(own, 2, False)
    across = hop(own, 0, True)
    down_across, up_across = hop(down, 0, True), hop(up, 0, True)
    far_across = hop(across, 2, False)
    chunks = [far, up, across, down_across, own, down, up_across, far_across]
    others = [swap(c) for c in chunks]

    target = aims_of(positive)
    scores, keep, send, q_tile, p_tile = scores_of(chunks, others, target)
    q_flip = flipped(q_tile)
    stats = merge([keep, swap(send)])
    stats = merge([stats, hop(stats, 0, True)], (q_flip,))
    own_lse, part = merge([stats, hop(stats, 2, False), hop(stats, 1, False), hop(stats, 3, False)], last=True)
    slope, part = slope_of(scores, target, own_lse, swap(own_lse), part)

    outs = grads_of(1, ((1, 3), (2,), (0,)), (slope, q_flip, p_tile, part), ())
    part = part + hop_xor(part, 1)
    keeps, recvs = outs[:3], [swap(s) for s in outs[3:6]]
    sides, beyond = join([keeps[0], recvs[0]]), join([keeps[1], recvs[1]])
    ready = (sides, beyond)
    sides, beyond = hop(sides, 0, True), hop(beyond, 2, False)
    across = [keeps[2], recvs[2]]
    part = part + hop(part, 2, False, 1)
    outs = grads_of(0, ((1,), (3,), (2,), (0,)), (slope, q_flip, p_tile, part), (ready[0], beyond, part))
    keeps, recvs = outs[:4], [swap(s) for s in outs[4:8]]
    up = hop(join([keeps[0], recvs[0], sides], pick=0), 1, False)
    down = hop(join([keeps[1], recvs[1], sides], pick=1), 3, False)
    across = hop(join([*across, beyond]), 0, True)
    far = hop(join([keeps[2], recvs[2]]), 2, False)
    home = join([keeps[3], recvs[3]])
    part = after(outs[8], across)
    part = part + hop(part, 0, True, 1)
    part = part + swap(part)
    mine, other = total([home, far, across, up, down], (part,))
    grad_queries, grad_passages = finish(mine, swap(other))
    loss = part[0, 0] / (32768.0 * log2_e)
    return loss, grad_queries, grad_passages


def solution(mesh):
    in_specs = (P(("row", "col"), None), P("col", "row"), P("row"))
    out_specs = (P(), P(("row", "col"), None), P("col", "row"))
    return jax.shard_map(shards, mesh=mesh, in_specs=in_specs, out_specs=out_specs, check_vma=False)
```

```python
import functools

import jax
import jax.numpy as jnp
from jax import lax
from jax.experimental import pallas as pl
from jax.experimental.pallas import tpu as pltpu
from jax.sharding import PartitionSpec as P

logit_scale = 40.0
log2_e = 1.4426950408889634
score_scale = logit_scale * log2_e
low = -1e30
AX = ("row", "col")
f32, bf16 = jnp.float32, jnp.bfloat16
MIB = 1024 * 1024


def lin(y, c, z, x):
    return ((y * 2 + c) * 4 + z) * 4 + x


def moves(step, turn):
    pairs = []
    for y in range(4):
        for z in range(4):
            for x in range(4):
                far_z, side = step(z, x, x ^ 1)
                pairs.append((lin(y, turn, z, x), lin(y, turn, far_z, side)))
                far_y, side = step(y, x, 3 - x)
                pairs.append((lin(y, 1 - turn, z, x), lin(far_y, 1 - turn, z, side)))
    return pairs


def hop(a, d, flip, turn=0):
    return lax.ppermute(a, AX, moves(lambda r, x, other: ((r + d) % 4, other if flip else x), turn))


def hop_xor(a, turn=0):
    return lax.ppermute(a, AX, moves(lambda r, x, other: (r ^ 1, x), turn))


def swap(a):
    return lax.ppermute(a, "row", [(i, i ^ 1) for i in range(8)])


def place():
    row, col = lax.axis_index("row"), lax.axis_index("col")
    return row // 2, row % 2, col // 4, col % 4


OFFSETS = [(2, 0), (1, 0), (0, 1), (3, 1), (0, 0), (3, 0), (1, 1), (2, 1)]


def load_copies(core, y, z, x, mine, theirs, q_dst, p_dst, sems):
    out = []
    for k, (d, flip) in enumerate(OFFSETS):
        slot = ((x % 2) ^ flip) * 4 + (z - d + 4) % 4
        far_y = (y - d + 4) % 4
        rank = (x // 2) ^ flip
        for which in range(2):
            copies = []
            q_src, p_src = (mine[k], theirs[k]) if which == 0 else (theirs[k], mine[k])
            if q_dst is not None:
                rows = pl.ds(pl.multiple_of(slot * 128, 128), 128)
                copies.append(pltpu.make_async_copy(q_src.at[which], q_dst.at[rows], sems.at[k, 0]))
            if p_dst is not None:
                for part in range(2):
                    rows = pl.ds(pl.multiple_of(far_y * 256 + (1 - part) * 128, 128), 128)
                    copies.append(
                        pltpu.make_async_copy(p_src.at[part], p_dst.at[rank, rows], sems.at[k, 1 + part])
                    )
            out.append((which, copies))
    return out


def run_copies(core, groups, start):
    for which in range(2):

        @pl.when(core == which)
        def _():
            for w, copies in groups:
                if w == which:
                    for copy in copies:
                        copy.start() if start else copy.wait()


TILE = 32


def lane_groups():
    return [(g // 8, slice(g % 8 * 128, g % 8 * 128 + 128)) for g in range(16)]


def fold(a):
    return sum(a[r : r + 8] for r in range(0, a.shape[0], 8))


def score_kernel(*refs):
    mine, theirs, (target, sv, keep, send, qv, pt, row_top, row_sum, col_top, sems) = (
        refs[:8],
        refs[8:16],
        refs[16:],
    )
    y, core, z, x = place()
    groups = load_copies(core, y, z, x, mine, theirs, qv, pt, sems)
    run_copies(core, groups, True)
    run_copies(core, groups, False)
    for h in range(2):
        for n in range(2):
            cols = slice(n * 512, n * 512 + 512)
            s = score_scale * jnp.dot(qv[...], pt[h, :, cols], preferred_element_type=f32)
            sv[h, :, cols] = s
            col_top[h, :, cols] = jnp.broadcast_to(jnp.max(s, axis=0, keepdims=True), (8, 512))
            top = jnp.maximum(
                jnp.maximum(s[:, :128], s[:, 128:256]), jnp.maximum(s[:, 256:384], s[:, 384:])
            )
            row_top[...] = top if h == n == 0 else jnp.maximum(row_top[...], top)
    tops = []
    for s in range(8):
        rows = slice(s * 128, s * 128 + 128)
        top = jnp.max(row_top[rows, :].T, axis=0, keepdims=True)
        tops.append(top)
        row_top[rows, :] = jnp.broadcast_to(top, (128, 128)).T
    lanes = lax.broadcasted_iota(jnp.int32, (TILE, 128), 1).astype(f32)

    def step(i, carry):
        col_acc, hits = carry
        rows = pl.ds(pl.multiple_of(i * TILE, TILE), TILE)
        top, aim = row_top[rows, :], target[rows, :]
        total, cols = jnp.zeros((TILE, 128), f32), []
        for g, (h, at) in enumerate(lane_groups()):
            t = sv[h, rows, at]
            total = total + jnp.exp2(t - top)
            cols.append(col_acc[g] + fold(jnp.exp2(t - col_top[h, 0:1, at])))
            hits = hits + fold(jnp.where(lanes == aim - g * 128, t, 0.0))
        row_sum[rows, :] = total
        return tuple(cols), hits

    zero = jnp.zeros((8, 128), f32)
    col_acc, hits = lax.fori_loop(0, 1024 // TILE, step, ((zero,) * 16, zero))
    hits = jnp.sum(hits, axis=0, keepdims=True)

    def fill(rows_ref, cols_ref, first):
        off = 0 if first else 1024
        for s in range(8):
            at = slice(off + s * 128, off + s * 128 + 128)
            rows_ref[0:1, at] = tops[s]
            rows_ref[1:2, at] = jnp.sum(row_sum[s * 128 : s * 128 + 128, :].T, axis=0, keepdims=True)
        gap = slice(1024 - off, 2048 - off)
        rows_ref[0:1, gap] = jnp.full((1, 1024), low, f32)
        rows_ref[1:2, gap] = jnp.zeros((1, 1024), f32)
        rows_ref[2:3, :] = jnp.zeros((1, 2048), f32)
        rows_ref[2:3, :128] = hits
        for h in range(2):
            cols_ref[0:1, h * 1024 : h * 1024 + 1024] = col_top[h, 0:1, :]
        for g in range(16):
            cols_ref[1:2, g * 128 : g * 128 + 128] = jnp.sum(col_acc[g], axis=0, keepdims=True)
        cols_ref[2:3, :] = jnp.zeros((1, 2048), f32)

    @pl.when(core == 0)
    def _():
        fill(keep, send, True)

    @pl.when(core == 1)
    def _():
        fill(send, keep, False)


def slope_kernel(sv, target, own_lse, got_lse, slope, row_lse):
    first = place()[1] == 0
    mine_lse, their_lse = own_lse[...], got_lse[...]
    rows_lse = jnp.where(first, mine_lse[:, :1024], their_lse[:, 1024:])
    cols_lse = jnp.where(first, their_lse, mine_lse)
    for s in range(8):
        row_lse[s * 128 : s * 128 + 128, :] = jnp.broadcast_to(
            rows_lse[:, s * 128 : s * 128 + 128], (128, 128)
        ).T
    lanes = lax.broadcasted_iota(jnp.int32, (TILE, 128), 1).astype(f32)

    def step(i, carry):
        rows = pl.ds(pl.multiple_of(i * TILE, TILE), TILE)
        aim, lse = target[rows, :], row_lse[rows, :]
        for g, (h, at) in enumerate(lane_groups()):
            t = sv[h, rows, at]
            e = 0.5 * (jnp.exp2(t - lse) + jnp.exp2(t - cols_lse[:, g * 128 : g * 128 + 128]))
            slope[h, rows, at] = jnp.where(lanes == aim - g * 128, e - 1.0, e).astype(bf16)
        return carry

    lax.fori_loop(0, 1024 // TILE, step, 0)


def grad_kernel(flip, order, n_ties, *refs):
    n = len(order)
    steps = [(g, i, d) for g, group in enumerate(order) for i, d in enumerate(group)]
    (slope, qt, pt, part, far_part), refs = refs[:5], refs[5 + n_ties :]
    keeps, sends, (part_out, gq, gp, zeros, out_sems) = refs[:n], refs[n : 2 * n], refs[2 * n :]
    part_out[...] = part[...] + far_part[...]
    y, core, z, x = place()
    zeros[...] = jnp.zeros(zeros.shape, bf16)
    half = (x % 2) ^ flip
    rank = (x // 2) ^ flip
    rows = pl.ds(pl.multiple_of(half * 512, 512), 512)

    def send_queries(which):
        copies = []
        for k, (g, i, d) in enumerate(steps):
            to = (sends if which else keeps)[g].at[i]
            at = pl.ds(pl.multiple_of((z + d) % 4 * 128, 128), 128)
            copies.append(pltpu.make_async_copy(gq.at[at], to.at[which], out_sems.at[k, 0]))
            copies.append(pltpu.make_async_copy(zeros, to.at[1 - which], out_sems.at[k, 1]))
        return copies

    def send_passages(which, m, cut):
        copies = []
        for k, (g, i, d) in enumerate(steps):
            to = (keeps if which else sends)[g].at[i]
            for part in range(2):
                at = pl.ds(pl.multiple_of((y + d) % 4 * 256 + (1 - part) * 128, 128), 128)
                copies.append(
                    pltpu.make_async_copy(gp.at[at, cut], to.at[part, :, cut], out_sems.at[k, 2 + 2 * m + part])
                )
        return copies

    def start(make):
        for which in range(2):

            @pl.when(core == which)
            def _():
                for copy in make(which):
                    copy.start()

    for m in range(4):
        cut = slice(m * 256, m * 256 + 256)
        g = sum(
            lax.dot_general(
                slope[h, rows, :], pt[h, cut, :], (((1,), (1,)), ((), ())), preferred_element_type=f32
            )
            for h in range(2)
        )
        gq[:, cut] = (logit_scale * g).astype(bf16)
    start(send_queries)
    cuts = [slice(m * 512, m * 512 + 512) for m in range(2)]
    for m, cut in enumerate(cuts):
        g = jnp.dot(qt[...], slope[rank, :, cut], preferred_element_type=f32)
        gp[:, cut] = (logit_scale * g).astype(bf16)
        start(functools.partial(send_passages, m=m, cut=cut))

    for which in range(2):

        @pl.when(core == which)
        def _():
            for copy in send_queries(which) + [c for m, cut in enumerate(cuts) for c in send_passages(which, m, cut)]:
                copy.wait()


ANY = pl.BlockSpec(memory_space=pl.ANY)
VM = pl.BlockSpec(memory_space=pltpu.VMEM)


def arr(shape, dtype):
    return jax.ShapeDtypeStruct(shape, dtype)


def cost(flops, nbytes):
    return pl.CostEstimate(flops=flops, bytes_accessed=nbytes, transcendentals=0)


def scores_of(mine, theirs, target):
    return pl.pallas_call(
        score_kernel,
        out_shape=(
            arr((2, 1024, 1024), f32),
            arr((3, 2048), f32),
            arr((3, 2048), f32),
            arr((1024, 1024), bf16),
            arr((2, 1024, 1024), bf16),
        ),
        in_specs=[ANY] * 16 + [VM],
        out_specs=(VM,) * 5,
        scratch_shapes=[
            pltpu.VMEM((1024, 128), f32),
            pltpu.VMEM((1024, 128), f32),
            pltpu.VMEM((2, 8, 1024), f32),
            pltpu.SemaphoreType.DMA((8, 3)),
        ],
        compiler_params=pltpu.CompilerParams(vmem_limit_bytes=18 * MIB),
        cost_estimate=cost(2 * 1024**2 * 2048, 16 * MIB),
        name="scores",
    )(*mine, *theirs, target)


def flip_kernel(q, out):
    for m in range(8):
        out[:, m * 128 : m * 128 + 128] = q[m * 128 : m * 128 + 128, :].T


def flipped(q):
    return pl.pallas_call(
        flip_kernel,
        out_shape=arr(q.shape, bf16),
        in_specs=[VM],
        out_specs=VM,
        compiler_params=pltpu.CompilerParams(vmem_limit_bytes=8 * MIB),
        cost_estimate=cost(0, 4 * MIB),
        name="flip",
    )(q)


def entry_kernel(q_in, p_in, mine, send, q, p, sems):
    copies = [pltpu.make_async_copy(q_in, q, sems.at[0]), pltpu.make_async_copy(p_in, p, sems.at[1])]
    for copy in copies:
        copy.start()
    for copy in copies:
        copy.wait()
    first = place()[1] == 0
    flat = p[...].T
    mine[...] = jnp.where(first, q[...], flat)
    send[...] = jnp.where(first, flat, q[...])


def entry(q, p):
    return pl.pallas_call(
        entry_kernel,
        out_shape=[arr((128, 1024), bf16)] * 2,
        in_specs=[ANY] * 2,
        out_specs=[VM] * 2,
        scratch_shapes=[pltpu.VMEM(q.shape, bf16), pltpu.VMEM(p.shape, bf16), pltpu.SemaphoreType.DMA((2,))],
        compiler_params=pltpu.CompilerParams(vmem_limit_bytes=4 * MIB),
        cost_estimate=cost(0, MIB),
        name="entry",
    )(q, p)


def aim_kernel(positive, out):
    _, _, z, x = place()
    side = (x + 1) % 4 // 2
    for s in range(8):
        p = positive[pl.ds(s % 4 * 4 + x // 2 * 2 + s // 4, 1), :]
        far_z, far_x = p >> 12, (p >> 10) & 3
        inside = (far_z == z) & ((((far_x + 1) & 3) >> 1) == side)
        aim = jnp.where(inside, (far_x >> 1) * 1024 + (p & 1023), -1).astype(f32)
        out[s * 128 : s * 128 + 128, :] = jnp.broadcast_to(aim, (128, 128)).T


def aims_of(positive):
    return pl.pallas_call(
        aim_kernel,
        out_shape=arr((1024, 128), f32),
        in_specs=[VM],
        out_specs=VM,
        compiler_params=pltpu.CompilerParams(vmem_limit_bytes=4 * MIB),
        cost_estimate=cost(0, MIB),
        name="aims",
    )(positive.reshape(16, 128))


def after_kernel(a, *refs):
    refs[-1][...] = a[...]


def after(a, *ties):
    return pl.pallas_call(
        after_kernel,
        out_shape=arr(a.shape, a.dtype),
        in_specs=[VM] + [ANY] * len(ties),
        out_specs=VM,
        compiler_params=pltpu.CompilerParams(vmem_limit_bytes=4 * MIB),
        cost_estimate=cost(0, 1024),
        name="after",
    )(a, *ties)


def finish_kernel(mine, other, grad_queries, grad_passages):
    first = place()[1] == 0
    a, b = mine[...], other[...]
    grad_queries[...] = jnp.where(first, a, b)
    grad_passages[...] = jnp.where(first, b, a).T


def finish(mine, other):
    return pl.pallas_call(
        finish_kernel,
        out_shape=[arr((128, 1024), f32), arr((1024, 128), f32)],
        in_specs=[VM] * 2,
        out_specs=[VM] * 2,
        compiler_params=pltpu.CompilerParams(vmem_limit_bytes=8 * MIB),
        cost_estimate=cost(0, 2 * MIB),
        name="finish",
    )(mine, other)


def slope_of(scores, target, own_lse, got_lse):
    return pl.pallas_call(
        slope_kernel,
        out_shape=arr((2, 1024, 1024), bf16),
        in_specs=[VM] * 4,
        out_specs=VM,
        scratch_shapes=[pltpu.VMEM((1024, 128), f32)],
        compiler_params=pltpu.CompilerParams(vmem_limit_bytes=8 * MIB),
        cost_estimate=cost(2 * 1024**2 * 2048, 12 * MIB),
        name="slope",
    )(scores, target, own_lse, got_lse)


def grads_of(flip, order, operands, ties):
    chunks = [arr((len(group), 2, 128, 1024), bf16) for group in order]
    return pl.pallas_call(
        functools.partial(grad_kernel, flip, order, len(ties)),
        out_shape=chunks * 2 + [arr((8, 128), f32)],
        in_specs=[VM] * len(operands) + [ANY] * len(ties),
        out_specs=[VM] * (2 * len(chunks) + 1),
        scratch_shapes=[
            pltpu.VMEM((512, 1024), bf16),
            pltpu.VMEM((1024, 1024), bf16),
            pltpu.VMEM((128, 1024), bf16),
            pltpu.SemaphoreType.DMA((4, 6)),
        ],
        compiler_params=pltpu.CompilerParams(vmem_limit_bytes=12 * MIB),
        cost_estimate=cost(2 * 1024**2 * 2048, 20 * MIB),
        name="grads_far" if flip else "grads_near",
    )(*operands, *ties)


def join_kernel(picks, *refs):
    out = refs[-1]
    parts = [r[...] if p is None else r[p : p + 1] for p, r in zip(picks, refs)]
    out[...] = sum(p.astype(f32) for p in parts).astype(bf16)


def join(terms, ties=(), pick=None):
    a, n = terms[0], len(terms)
    return pl.pallas_call(
        functools.partial(join_kernel, [None] * (n - 1) + [pick]),
        out_shape=arr(a.shape, bf16),
        in_specs=[VM] * n + [ANY] * len(ties),
        out_specs=VM,
        compiler_params=pltpu.CompilerParams(vmem_limit_bytes=8 * MIB),
        cost_estimate=cost(a.size, 6 * a.size),
        name="join",
    )(*terms, *ties)


def total_kernel(n, *refs):
    mine, other = refs[-2:]
    mine[...] = sum(r[0, 0].astype(f32) for r in refs[:n])
    other[...] = sum(r[0, 1].astype(f32) for r in refs[:n])


def total(terms, ties=()):
    return pl.pallas_call(
        functools.partial(total_kernel, len(terms)),
        out_shape=[arr((128, 1024), f32)] * 2,
        in_specs=[VM] * len(terms) + [ANY] * len(ties),
        out_specs=[VM] * 2,
        compiler_params=pltpu.CompilerParams(vmem_limit_bytes=8 * MIB),
        cost_estimate=cost(5 * 2**18, 4 * MIB),
        name="total",
    )(*terms, *ties)


def merge_kernel(n, last, *refs):
    ins = refs[:n]
    top = ins[0][0:1]
    for a in ins[1:]:
        top = jnp.maximum(top, a[0:1])
    total = sum(a[1:2] * jnp.exp2(a[0:1] - top) for a in ins)
    hits = sum(a[2:3] for a in ins)
    if last:
        lse, part = refs[-2:]
        lse[...] = top + jnp.log2(total)
        figure = jnp.sum(lse[...] - 2.0 * hits, axis=1, keepdims=True)
        part[...] = jnp.broadcast_to(figure, (8, 128))
    else:
        out = refs[-1]
        out[0:1] = top
        out[1:2] = total
        out[2:3] = hits


def merge(ins, ties=(), last=False):
    return pl.pallas_call(
        functools.partial(merge_kernel, len(ins), last),
        out_shape=[arr((1, 2048), f32), arr((8, 128), f32)] if last else arr((3, 2048), f32),
        in_specs=[VM] * len(ins) + [ANY] * len(ties),
        out_specs=[VM, VM] if last else VM,
        compiler_params=pltpu.CompilerParams(vmem_limit_bytes=4 * MIB),
        cost_estimate=cost(0, 2**16),
        name="merge",
    )(*ins, *ties)


def shards(queries, passages, positive):
    mine, send = entry(queries, passages)
    own = jnp.stack([mine, swap(send)])
    down, up, far = hop(own, 3, False), hop(own, 1, False), hop(own, 2, False)
    across = hop(own, 0, True)
    down_across, up_across = hop(down, 0, True), hop(up, 0, True)
    far_across = hop(across, 2, False)
    chunks = [far, up, across, down_across, own, down, up_across, far_across]
    others = [swap(c) for c in chunks]

    target = aims_of(positive)
    scores, keep, send, q_tile, p_tile = scores_of(chunks, others, target)
    q_flip = flipped(q_tile)
    stats = merge([keep, swap(send)])
    stats = merge([stats, hop(stats, 0, True)], (q_flip,))
    own_lse, part = merge([stats, hop(stats, 2, False), hop(stats, 1, False), hop(stats, 3, False)], last=True)
    slope = slope_of(scores, target, own_lse, swap(own_lse))

    outs = grads_of(1, ((1, 3), (2,), (0,)), (slope, q_flip, p_tile, part, hop_xor(part, 1)), ())
    keeps, recvs, part = outs[:3], [swap(s) for s in outs[3:6]], outs[6]
    sides, beyond = join([keeps[0], recvs[0]]), join([keeps[1], recvs[1]])
    ready = (sides, beyond)
    sides, beyond = hop(sides, 0, True), hop(beyond, 2, False)
    across = [keeps[2], recvs[2]]
    outs = grads_of(0, ((1,), (3,), (2,), (0,)), (slope, q_flip, p_tile, part, hop(part, 2, False, 1)), ready)
    part = outs[8]
    keeps, recvs = outs[:4], [swap(s) for s in outs[4:8]]
    far = join([keeps[2], recvs[2]])
    up = join([keeps[0], recvs[0], sides], (far,), pick=0)
    down = join([keeps[1], recvs[1], sides], (far,), pick=1)
    across = hop(join([*across, beyond], (far,)), 0, True)
    far, up, down = hop(far, 2, False), hop(up, 1, False), hop(down, 3, False)
    home = join([keeps[3], recvs[3]])
    part = after(part, far)
    part = part + hop(part, 0, True, 1)
    part = part + swap(part)
    mine, other = total([home, far, across, up, down], (part,))
    grad_queries, grad_passages = finish(mine, swap(other))
    loss = part[0, 0] / (32768.0 * log2_e)
    return loss, grad_queries, grad_passages


def solution(mesh):
    in_specs = (P(("row", "col"), None), P("col", "row"), P("row"))
    out_specs = (P(), P(("row", "col"), None), P("col", "row"))
    return jax.shard_map(shards, mesh=mesh, in_specs=in_specs, out_specs=out_specs, check_vma=False)
```

```python
import functools

import jax
import jax.numpy as jnp
from jax import lax
from jax.experimental import pallas as pl
from jax.experimental.pallas import tpu as pltpu
from jax.sharding import PartitionSpec as P

logit_scale = 40.0
log2_e = 1.4426950408889634
score_scale = logit_scale * log2_e
low = -1e30
AX = ("row", "col")
f32, bf16 = jnp.float32, jnp.bfloat16
MIB = 1024 * 1024


def lin(y, c, z, x):
    return ((y * 2 + c) * 4 + z) * 4 + x


def moves(step, turn):
    pairs = []
    for y in range(4):
        for z in range(4):
            for x in range(4):
                far_z, side = step(z, x, x ^ 1)
                pairs.append((lin(y, turn, z, x), lin(y, turn, far_z, side)))
                far_y, side = step(y, x, 3 - x)
                pairs.append((lin(y, 1 - turn, z, x), lin(far_y, 1 - turn, z, side)))
    return pairs


def hop(a, d, flip, turn=0):
    return lax.ppermute(a, AX, moves(lambda r, x, other: ((r + d) % 4, other if flip else x), turn))


def hop_xor(a, turn=0):
    return lax.ppermute(a, AX, moves(lambda r, x, other: (r ^ 1, x), turn))


def swap(a):
    return lax.ppermute(a, "row", [(i, i ^ 1) for i in range(8)])


def place():
    row, col = lax.axis_index("row"), lax.axis_index("col")
    return row // 2, row % 2, col // 4, col % 4


OFFSETS = [(0, 0), (3, 1), (2, 0), (3, 0), (2, 1), (1, 1), (1, 0), (0, 1)]


def load_copies(core, y, z, x, mine, theirs, q_dst, p_dst, sems):
    out = []
    for k, (d, flip) in enumerate(OFFSETS):
        slot = ((x % 2) ^ flip) * 4 + (z - d + 4) % 4
        far_y = (y - d + 4) % 4
        rank = (x // 2) ^ flip
        for which in range(2):
            copies = []
            q_src, p_src = (mine[k], theirs[k]) if which == 0 else (theirs[k], mine[k])
            if q_dst is not None:
                rows = pl.ds(pl.multiple_of(slot * 128, 128), 128)
                copies.append(pltpu.make_async_copy(q_src.at[which], q_dst.at[rows], sems.at[k, 0]))
            if p_dst is not None:
                for part in range(2):
                    rows = pl.ds(pl.multiple_of(far_y * 256 + (1 - part) * 128, 128), 128)
                    copies.append(
                        pltpu.make_async_copy(p_src.at[part], p_dst.at[rank, rows], sems.at[k, 1 + part])
                    )
            out.append((which, copies))
    return out


def run_copies(core, groups, start):
    for which in range(2):

        @pl.when(core == which)
        def _():
            for w, copies in groups:
                if w == which:
                    for copy in copies:
                        copy.start() if start else copy.wait()


TILE = 32


def lane_groups():
    return [(g // 8, slice(g % 8 * 128, g % 8 * 128 + 128)) for g in range(16)]


def fold(a):
    return sum(a[r : r + 8] for r in range(0, a.shape[0], 8))


def score_kernel(*refs):
    mine, theirs, (target, sv, keep, send, qv, pt, row_top, row_sum, col_top, sems) = (
        refs[:8],
        refs[8:16],
        refs[16:],
    )
    y, core, z, x = place()
    groups = load_copies(core, y, z, x, mine, theirs, qv, pt, sems)
    run_copies(core, groups, True)
    run_copies(core, groups, False)
    for h in range(2):
        for n in range(2):
            cols = slice(n * 512, n * 512 + 512)
            s = score_scale * jnp.dot(qv[...], pt[h, :, cols], preferred_element_type=f32)
            sv[h, :, cols] = s
            col_top[h, :, cols] = jnp.broadcast_to(jnp.max(s, axis=0, keepdims=True), (8, 512))
            top = jnp.maximum(
                jnp.maximum(s[:, :128], s[:, 128:256]), jnp.maximum(s[:, 256:384], s[:, 384:])
            )
            row_top[...] = top if h == n == 0 else jnp.maximum(row_top[...], top)
    tops = []
    for s in range(8):
        rows = slice(s * 128, s * 128 + 128)
        top = jnp.max(row_top[rows, :].T, axis=0, keepdims=True)
        tops.append(top)
        row_top[rows, :] = jnp.broadcast_to(top, (128, 128)).T
    lanes = lax.broadcasted_iota(jnp.int32, (TILE, 128), 1).astype(f32)

    def step(i, carry):
        col_acc, hits = carry
        rows = pl.ds(pl.multiple_of(i * TILE, TILE), TILE)
        top, aim = row_top[rows, :], target[rows, :]
        total, cols = jnp.zeros((TILE, 128), f32), []
        for g, (h, at) in enumerate(lane_groups()):
            t = sv[h, rows, at]
            total = total + jnp.exp2(t - top)
            cols.append(col_acc[g] + fold(jnp.exp2(t - col_top[h, 0:1, at])))
            hits = hits + fold(jnp.where(lanes == aim - g * 128, t, 0.0))
        row_sum[rows, :] = total
        return tuple(cols), hits

    zero = jnp.zeros((8, 128), f32)
    col_acc, hits = lax.fori_loop(0, 1024 // TILE, step, ((zero,) * 16, zero))
    hits = jnp.sum(hits, axis=0, keepdims=True)

    def fill(rows_ref, cols_ref, first):
        off = 0 if first else 1024
        for s in range(8):
            at = slice(off + s * 128, off + s * 128 + 128)
            rows_ref[0:1, at] = tops[s]
            rows_ref[1:2, at] = jnp.sum(row_sum[s * 128 : s * 128 + 128, :].T, axis=0, keepdims=True)
        gap = slice(1024 - off, 2048 - off)
        rows_ref[0:1, gap] = jnp.full((1, 1024), low, f32)
        rows_ref[1:2, gap] = jnp.zeros((1, 1024), f32)
        rows_ref[2:3, :] = jnp.zeros((1, 2048), f32)
        rows_ref[2:3, :128] = hits
        for h in range(2):
            cols_ref[0:1, h * 1024 : h * 1024 + 1024] = col_top[h, 0:1, :]
        for g in range(16):
            cols_ref[1:2, g * 128 : g * 128 + 128] = jnp.sum(col_acc[g], axis=0, keepdims=True)
        cols_ref[2:3, :] = jnp.zeros((1, 2048), f32)

    @pl.when(core == 0)
    def _():
        fill(keep, send, True)

    @pl.when(core == 1)
    def _():
        fill(send, keep, False)


def slope_kernel(sv, target, own_lse, got_lse, slope, row_lse):
    first = place()[1] == 0
    mine_lse, their_lse = own_lse[...], got_lse[...]
    rows_lse = jnp.where(first, mine_lse[:, :1024], their_lse[:, 1024:])
    cols_lse = jnp.where(first, their_lse, mine_lse)
    for s in range(8):
        row_lse[s * 128 : s * 128 + 128, :] = jnp.broadcast_to(
            rows_lse[:, s * 128 : s * 128 + 128], (128, 128)
        ).T
    lanes = lax.broadcasted_iota(jnp.int32, (TILE, 128), 1).astype(f32)

    def step(i, carry):
        rows = pl.ds(pl.multiple_of(i * TILE, TILE), TILE)
        aim, lse = target[rows, :], row_lse[rows, :]
        for g, (h, at) in enumerate(lane_groups()):
            t = sv[h, rows, at]
            e = 0.5 * (jnp.exp2(t - lse) + jnp.exp2(t - cols_lse[:, g * 128 : g * 128 + 128]))
            slope[h, rows, at] = jnp.where(lanes == aim - g * 128, e - 1.0, e).astype(bf16)
        return carry

    lax.fori_loop(0, 1024 // TILE, step, 0)


def grad_kernel(flip, order, n_parts, n_ties, *refs):
    n = len(order)
    steps = [(g, i, d) for g, group in enumerate(order) for i, d in enumerate(group)]
    (slope, qt, pt), parts, refs = refs[:3], refs[3 : 3 + n_parts], refs[3 + n_parts + n_ties :]
    keeps, sends, (part_out, gq, gp, zeros, out_sems) = refs[:n], refs[n : 2 * n], refs[2 * n :]
    part_out[...] = sum((p[...] for p in parts), jnp.zeros((8, 128), f32))
    y, core, z, x = place()
    zeros[...] = jnp.zeros(zeros.shape, bf16)
    half = (x % 2) ^ flip
    rank = (x // 2) ^ flip
    whole = len(steps) == 4

    def q_rows(k, d):
        return (z + d) % 4 * 128 if whole else k * 128

    def p_rows(k, d):
        return (y + d) % 4 * 256 if whole else k * 256

    def slope_rows(h):
        if whole:
            return slope[h, pl.ds(pl.multiple_of(half * 512, 512), 512), :]
        starts = [pl.multiple_of(half * 512 + (z + d) % 4 * 128, 128) for _, _, d in steps]
        return jnp.concatenate([slope[h, pl.ds(r, 128), :] for r in starts], axis=0)

    def q_flip_rows():
        if whole:
            return qt[...]
        starts = [pl.multiple_of((y + d) % 4 * 256, 256) for _, _, d in steps]
        return jnp.concatenate([qt[pl.ds(r, 256), :] for r in starts], axis=0)


    def send_queries(which):
        copies = []
        for k, (g, i, d) in enumerate(steps):
            to = (sends if which else keeps)[g].at[i]
            at = pl.ds(pl.multiple_of(q_rows(k, d), 128), 128)
            copies.append(pltpu.make_async_copy(gq.at[at], to.at[which], out_sems.at[k, 0]))
            copies.append(pltpu.make_async_copy(zeros, to.at[1 - which], out_sems.at[k, 1]))
        return copies

    def send_passages(which, m, cut):
        copies = []
        for k, (g, i, d) in enumerate(steps):
            to = (keeps if which else sends)[g].at[i]
            for part in range(2):
                at = pl.ds(pl.multiple_of(p_rows(k, d) + (1 - part) * 128, 128), 128)
                copies.append(
                    pltpu.make_async_copy(gp.at[at, cut], to.at[part, :, cut], out_sems.at[k, 2 + 2 * m + part])
                )
        return copies

    def start(make):
        for which in range(2):

            @pl.when(core == which)
            def _():
                for copy in make(which):
                    copy.start()

    for m in range(4):
        cut = slice(m * 256, m * 256 + 256)
        g = sum(
            lax.dot_general(
                slope_rows(h), pt[h, cut, :], (((1,), (1,)), ((), ())), preferred_element_type=f32
            )
            for h in range(2)
        )
        gq[:, cut] = (logit_scale * g).astype(bf16)
    start(send_queries)
    cuts = [slice(m * 512, m * 512 + 512) for m in range(2)]
    for m, cut in enumerate(cuts):
        g = jnp.dot(q_flip_rows(), slope[rank, :, cut], preferred_element_type=f32)
        gp[:, cut] = (logit_scale * g).astype(bf16)
        start(functools.partial(send_passages, m=m, cut=cut))

    for which in range(2):

        @pl.when(core == which)
        def _():
            for copy in send_queries(which) + [c for m, cut in enumerate(cuts) for c in send_passages(which, m, cut)]:
                copy.wait()


ANY = pl.BlockSpec(memory_space=pl.ANY)
VM = pl.BlockSpec(memory_space=pltpu.VMEM)


def arr(shape, dtype):
    return jax.ShapeDtypeStruct(shape, dtype)


def cost(flops, nbytes):
    return pl.CostEstimate(flops=flops, bytes_accessed=nbytes, transcendentals=0)


def scores_of(mine, theirs, target):
    return pl.pallas_call(
        score_kernel,
        out_shape=(
            arr((2, 1024, 1024), f32),
            arr((3, 2048), f32),
            arr((3, 2048), f32),
            arr((1024, 1024), bf16),
            arr((2, 1024, 1024), bf16),
        ),
        in_specs=[ANY] * 16 + [VM],
        out_specs=(VM,) * 5,
        scratch_shapes=[
            pltpu.VMEM((1024, 128), f32),
            pltpu.VMEM((1024, 128), f32),
            pltpu.VMEM((2, 8, 1024), f32),
            pltpu.SemaphoreType.DMA((8, 3)),
        ],
        compiler_params=pltpu.CompilerParams(vmem_limit_bytes=18 * MIB),
        cost_estimate=cost(2 * 1024**2 * 2048, 16 * MIB),
        name="scores",
    )(*mine, *theirs, target)


def flip_kernel(q, out):
    for m in range(8):
        out[:, m * 128 : m * 128 + 128] = q[m * 128 : m * 128 + 128, :].T


def flipped(q):
    return pl.pallas_call(
        flip_kernel,
        out_shape=arr(q.shape, bf16),
        in_specs=[VM],
        out_specs=VM,
        compiler_params=pltpu.CompilerParams(vmem_limit_bytes=8 * MIB),
        cost_estimate=cost(0, 4 * MIB),
        name="flip",
    )(q)


def entry_kernel(q_in, p_in, mine, send, q, p, sems):
    copies = [pltpu.make_async_copy(q_in, q, sems.at[0]), pltpu.make_async_copy(p_in, p, sems.at[1])]
    for copy in copies:
        copy.start()
    for copy in copies:
        copy.wait()
    first = place()[1] == 0
    flat = p[...].T
    mine[...] = jnp.where(first, q[...], flat)
    send[...] = jnp.where(first, flat, q[...])


def entry(q, p):
    return pl.pallas_call(
        entry_kernel,
        out_shape=[arr((128, 1024), bf16)] * 2,
        in_specs=[ANY] * 2,
        out_specs=[VM] * 2,
        scratch_shapes=[pltpu.VMEM(q.shape, bf16), pltpu.VMEM(p.shape, bf16), pltpu.SemaphoreType.DMA((2,))],
        compiler_params=pltpu.CompilerParams(vmem_limit_bytes=4 * MIB),
        cost_estimate=cost(0, MIB),
        name="entry",
    )(q, p)


def aim_kernel(positive, out):
    _, _, z, x = place()
    side = (x + 1) % 4 // 2
    for s in range(8):
        p = positive[pl.ds(s % 4 * 4 + x // 2 * 2 + s // 4, 1), :]
        far_z, far_x = p >> 12, (p >> 10) & 3
        inside = (far_z == z) & ((((far_x + 1) & 3) >> 1) == side)
        aim = jnp.where(inside, (far_x >> 1) * 1024 + (p & 1023), -1).astype(f32)
        out[s * 128 : s * 128 + 128, :] = jnp.broadcast_to(aim, (128, 128)).T


def aims_of(positive):
    return pl.pallas_call(
        aim_kernel,
        out_shape=arr((1024, 128), f32),
        in_specs=[VM],
        out_specs=VM,
        compiler_params=pltpu.CompilerParams(vmem_limit_bytes=4 * MIB),
        cost_estimate=cost(0, MIB),
        name="aims",
    )(positive.reshape(16, 128))


def after_kernel(a, *refs):
    refs[-1][...] = a[...]


def after(a, *ties):
    return pl.pallas_call(
        after_kernel,
        out_shape=arr(a.shape, a.dtype),
        in_specs=[VM] + [ANY] * len(ties),
        out_specs=VM,
        compiler_params=pltpu.CompilerParams(vmem_limit_bytes=4 * MIB),
        cost_estimate=cost(0, 1024),
        name="after",
    )(a, *ties)


def finish_kernel(mine, other, grad_queries, grad_passages):
    first = place()[1] == 0
    a, b = mine[...], other[...]
    grad_queries[...] = jnp.where(first, a, b)
    grad_passages[...] = jnp.where(first, b, a).T


def finish(mine, other):
    return pl.pallas_call(
        finish_kernel,
        out_shape=[arr((128, 1024), f32), arr((1024, 128), f32)],
        in_specs=[VM] * 2,
        out_specs=[VM] * 2,
        compiler_params=pltpu.CompilerParams(vmem_limit_bytes=8 * MIB),
        cost_estimate=cost(0, 2 * MIB),
        name="finish",
    )(mine, other)


def slope_of(scores, target, own_lse, got_lse):
    return pl.pallas_call(
        slope_kernel,
        out_shape=arr((2, 1024, 1024), bf16),
        in_specs=[VM] * 4,
        out_specs=VM,
        scratch_shapes=[pltpu.VMEM((1024, 128), f32)],
        compiler_params=pltpu.CompilerParams(vmem_limit_bytes=8 * MIB),
        cost_estimate=cost(2 * 1024**2 * 2048, 12 * MIB),
        name="slope",
    )(scores, target, own_lse, got_lse)


def grads_of(flip, order, operands, parts, ties):
    n = sum(len(group) for group in order)
    operands = (*operands, *parts)
    chunks = [arr((len(group), 2, 128, 1024), bf16) for group in order]
    return pl.pallas_call(
        functools.partial(grad_kernel, flip, order, len(parts), len(ties)),
        out_shape=chunks * 2 + [arr((8, 128), f32)],
        in_specs=[VM] * len(operands) + [ANY] * len(ties),
        out_specs=[VM] * (2 * len(chunks) + 1),
        scratch_shapes=[
            pltpu.VMEM((n * 128, 1024), bf16),
            pltpu.VMEM((n * 256, 1024), bf16),
            pltpu.VMEM((128, 1024), bf16),
            pltpu.SemaphoreType.DMA((n, 6)),
        ],
        compiler_params=pltpu.CompilerParams(vmem_limit_bytes=12 * MIB),
        cost_estimate=cost(n * 1024**3, n * 5 * MIB),
        name="grads_far" if flip else "grads_near",
    )(*operands, *ties)


def join_kernel(picks, *refs):
    out = refs[-1]
    parts = [r[...] if p is None else r[p : p + 1] for p, r in zip(picks, refs)]
    out[...] = sum(p.astype(f32) for p in parts).astype(bf16)


def join(terms, ties=(), pick=None):
    a, n = terms[0], len(terms)
    return pl.pallas_call(
        functools.partial(join_kernel, [None] * (n - 1) + [pick]),
        out_shape=arr(a.shape, bf16),
        in_specs=[VM] * n + [ANY] * len(ties),
        out_specs=VM,
        compiler_params=pltpu.CompilerParams(vmem_limit_bytes=8 * MIB),
        cost_estimate=cost(a.size, 6 * a.size),
        name="join",
    )(*terms, *ties)


def total_kernel(n, *refs):
    mine, other = refs[-2:]
    mine[...] = sum(r[0, 0].astype(f32) for r in refs[:n])
    other[...] = sum(r[0, 1].astype(f32) for r in refs[:n])


def total(terms, ties=()):
    return pl.pallas_call(
        functools.partial(total_kernel, len(terms)),
        out_shape=[arr((128, 1024), f32)] * 2,
        in_specs=[VM] * len(terms) + [ANY] * len(ties),
        out_specs=[VM] * 2,
        compiler_params=pltpu.CompilerParams(vmem_limit_bytes=8 * MIB),
        cost_estimate=cost(5 * 2**18, 4 * MIB),
        name="total",
    )(*terms, *ties)


def merge_kernel(n, last, *refs):
    ins = refs[:n]
    top = ins[0][0:1]
    for a in ins[1:]:
        top = jnp.maximum(top, a[0:1])
    total = sum(a[1:2] * jnp.exp2(a[0:1] - top) for a in ins)
    hits = sum(a[2:3] for a in ins)
    if last:
        lse, part = refs[-2:]
        lse[...] = top + jnp.log2(total)
        figure = jnp.sum(lse[...] - 2.0 * hits, axis=1, keepdims=True)
        part[...] = jnp.broadcast_to(figure, (8, 128))
    else:
        out = refs[-1]
        out[0:1] = top
        out[1:2] = total
        out[2:3] = hits


def merge(ins, ties=(), last=False):
    return pl.pallas_call(
        functools.partial(merge_kernel, len(ins), last),
        out_shape=[arr((1, 2048), f32), arr((8, 128), f32)] if last else arr((3, 2048), f32),
        in_specs=[VM] * len(ins) + [ANY] * len(ties),
        out_specs=[VM, VM] if last else VM,
        compiler_params=pltpu.CompilerParams(vmem_limit_bytes=4 * MIB),
        cost_estimate=cost(0, 2**16),
        name="merge",
    )(*ins, *ties)


def shards(queries, passages, positive):
    mine, send = entry(queries, passages)
    own = jnp.stack([mine, swap(send)])
    down, up, far = hop(own, 3, False), hop(own, 1, False), hop(own, 2, False)
    across = hop(own, 0, True)
    down_across, up_across = hop(down, 0, True), hop(up, 0, True)
    far_across = hop(across, 2, False)
    chunks = [own, down_across, far, down, far_across, up_across, up, across]
    others = [swap(c) for c in chunks]

    target = aims_of(positive)
    scores, keep, send, q_tile, p_tile = scores_of(chunks, others, target)
    q_flip = flipped(q_tile)
    stats = merge([keep, swap(send)])
    stats = merge([stats, hop(stats, 0, True)], (q_flip,))
    own_lse, part = merge([stats, hop(stats, 2, False), hop(stats, 1, False), hop(stats, 3, False)], last=True)
    slope = slope_of(scores, target, own_lse, swap(own_lse))

    tiles = (slope, q_flip, p_tile)
    outs = grads_of(1, ((1, 3),), tiles, (part, hop_xor(part, 1)), ())
    sides, part = join([outs[0], swap(outs[1])]), outs[2]
    outs = grads_of(1, ((2,), (0,)), tiles, (part,), ())
    moved = hop(part, 2, False, 1)
    beyond, across, part = join([outs[0], swap(outs[2])]), [outs[1], swap(outs[3])], outs[4]
    ready = (sides, beyond)
    sides, beyond = hop(sides, 0, True), hop(beyond, 2, False)
    outs = grads_of(0, ((2,), (0,)), tiles, (part, moved), ready)
    far = join([outs[0], swap(outs[2])])
    home = join([outs[1], swap(outs[3])])
    outs = grads_of(0, ((1,), (3,)), tiles, (outs[4],), ())
    part = outs[4]
    up = join([outs[0], swap(outs[2]), sides], (), pick=0)
    down = join([outs[1], swap(outs[3]), sides], (), pick=1)
    across = hop(join([*across, beyond], ()), 0, True)
    far, up, down = hop(far, 2, False), hop(up, 1, False), hop(down, 3, False)
    part = after(part, far)
    part = part + hop(part, 0, True, 1)
    part = part + swap(part)
    mine, other = total([home, far, across, up, down], (part,))
    grad_queries, grad_passages = finish(mine, swap(other))
    loss = part[0, 0] / (32768.0 * log2_e)
    return loss, grad_queries, grad_passages


def solution(mesh):
    in_specs = (P(("row", "col"), None), P("col", "row"), P("row"))
    out_specs = (P(), P(("row", "col"), None), P("col", "row"))
    return jax.shard_map(shards, mesh=mesh, in_specs=in_specs, out_specs=out_specs, check_vma=False)
```

```python
import functools

import jax
import jax.numpy as jnp
from jax import lax
from jax.experimental import pallas as pl
from jax.experimental.pallas import tpu as pltpu
from jax.sharding import PartitionSpec as P

logit_scale = 40.0
log2_e = 1.4426950408889634
score_scale = logit_scale * log2_e
low = -1e30
AX = ("row", "col")
f32, bf16 = jnp.float32, jnp.bfloat16
MIB = 1024 * 1024


def lin(y, c, z, x):
    return ((y * 2 + c) * 4 + z) * 4 + x


def moves(step, turn):
    pairs = []
    for y in range(4):
        for z in range(4):
            for x in range(4):
                far_z, side = step(z, x, x ^ 1)
                pairs.append((lin(y, turn, z, x), lin(y, turn, far_z, side)))
                far_y, side = step(y, x, 3 - x)
                pairs.append((lin(y, 1 - turn, z, x), lin(far_y, 1 - turn, z, side)))
    return pairs


def hop(a, d, flip, turn=0):
    return lax.ppermute(a, AX, moves(lambda r, x, other: ((r + d) % 4, other if flip else x), turn))


def hop_xor(a, turn=0):
    return lax.ppermute(a, AX, moves(lambda r, x, other: (r ^ 1, x), turn))


def swap(a):
    return lax.ppermute(a, "row", [(i, i ^ 1) for i in range(8)])


def place():
    row, col = lax.axis_index("row"), lax.axis_index("col")
    return row // 2, row % 2, col // 4, col % 4


OFFSETS = [(3, 1), (2, 1), (2, 0), (0, 0), (0, 1), (1, 1), (3, 0), (1, 0)]


def load_copies(core, y, z, x, mine, theirs, q_dst, p_dst, sems):
    out = []
    for k, (d, flip) in enumerate(OFFSETS):
        slot = ((x % 2) ^ flip) * 4 + (z - d + 4) % 4
        far_y = (y - d + 4) % 4
        rank = (x // 2) ^ flip
        for which in range(2):
            copies = []
            q_src, p_src = (mine[k], theirs[k]) if which == 0 else (theirs[k], mine[k])
            if q_dst is not None:
                rows = pl.ds(pl.multiple_of(slot * 128, 128), 128)
                copies.append(pltpu.make_async_copy(q_src.at[which], q_dst.at[rows], sems.at[k, 0]))
            if p_dst is not None:
                for part in range(2):
                    rows = pl.ds(pl.multiple_of(far_y * 256 + (1 - part) * 128, 128), 128)
                    copies.append(
                        pltpu.make_async_copy(p_src.at[part], p_dst.at[rank, rows], sems.at[k, 1 + part])
                    )
            out.append((which, copies))
    return out


def run_copies(core, groups, start):
    for which in range(2):

        @pl.when(core == which)
        def _():
            for w, copies in groups:
                if w == which:
                    for copy in copies:
                        copy.start() if start else copy.wait()


TILE = 32


def lane_groups():
    return [(g // 8, slice(g % 8 * 128, g % 8 * 128 + 128)) for g in range(16)]


def fold(a):
    return sum(a[r : r + 8] for r in range(0, a.shape[0], 8))


def score_kernel(*refs):
    mine, theirs, (target, sv, keep, send, qv, pt, row_top, row_sum, col_top, sems) = (
        refs[:8],
        refs[8:16],
        refs[16:],
    )
    y, core, z, x = place()
    groups = load_copies(core, y, z, x, mine, theirs, qv, pt, sems)
    run_copies(core, groups, True)
    run_copies(core, groups, False)
    for h in range(2):
        for n in range(2):
            cols = slice(n * 512, n * 512 + 512)
            s = score_scale * jnp.dot(qv[...], pt[h, :, cols], preferred_element_type=f32)
            sv[h, :, cols] = s
            col_top[h, :, cols] = jnp.broadcast_to(jnp.max(s, axis=0, keepdims=True), (8, 512))
            top = jnp.maximum(
                jnp.maximum(s[:, :128], s[:, 128:256]), jnp.maximum(s[:, 256:384], s[:, 384:])
            )
            row_top[...] = top if h == n == 0 else jnp.maximum(row_top[...], top)
    tops = []
    for s in range(8):
        rows = slice(s * 128, s * 128 + 128)
        top = jnp.max(row_top[rows, :].T, axis=0, keepdims=True)
        tops.append(top)
        row_top[rows, :] = jnp.broadcast_to(top, (128, 128)).T
    lanes = lax.broadcasted_iota(jnp.int32, (TILE, 128), 1).astype(f32)

    def step(i, carry):
        col_acc, hits = carry
        rows = pl.ds(pl.multiple_of(i * TILE, TILE), TILE)
        top, aim = row_top[rows, :], target[rows, :]
        total, cols = jnp.zeros((TILE, 128), f32), []
        for g, (h, at) in enumerate(lane_groups()):
            t = sv[h, rows, at]
            total = total + jnp.exp2(t - top)
            cols.append(col_acc[g] + fold(jnp.exp2(t - col_top[h, 0:1, at])))
            hits = hits + fold(jnp.where(lanes == aim - g * 128, t, 0.0))
        row_sum[rows, :] = total
        return tuple(cols), hits

    zero = jnp.zeros((8, 128), f32)
    col_acc, hits = lax.fori_loop(0, 1024 // TILE, step, ((zero,) * 16, zero), unroll=2)
    hits = jnp.sum(hits, axis=0, keepdims=True)

    def fill(rows_ref, cols_ref, first):
        off = 0 if first else 1024
        for s in range(8):
            at = slice(off + s * 128, off + s * 128 + 128)
            rows_ref[0:1, at] = tops[s]
            rows_ref[1:2, at] = jnp.sum(row_sum[s * 128 : s * 128 + 128, :].T, axis=0, keepdims=True)
        gap = slice(1024 - off, 2048 - off)
        rows_ref[0:1, gap] = jnp.full((1, 1024), low, f32)
        rows_ref[1:2, gap] = jnp.zeros((1, 1024), f32)
        rows_ref[2:3, :] = jnp.zeros((1, 2048), f32)
        rows_ref[2:3, :128] = hits
        for h in range(2):
            cols_ref[0:1, h * 1024 : h * 1024 + 1024] = col_top[h, 0:1, :]
        for g in range(16):
            cols_ref[1:2, g * 128 : g * 128 + 128] = jnp.sum(col_acc[g], axis=0, keepdims=True)
        cols_ref[2:3, :] = jnp.zeros((1, 2048), f32)

    @pl.when(core == 0)
    def _():
        fill(keep, send, True)

    @pl.when(core == 1)
    def _():
        fill(send, keep, False)


def slope_kernel(sv, target, own_lse, got_lse, slope, row_lse):
    first = place()[1] == 0
    mine_lse, their_lse = own_lse[...], got_lse[...]
    rows_lse = jnp.where(first, mine_lse[:, :1024], their_lse[:, 1024:])
    cols_lse = jnp.where(first, their_lse, mine_lse)
    for s in range(8):
        row_lse[s * 128 : s * 128 + 128, :] = jnp.broadcast_to(
            rows_lse[:, s * 128 : s * 128 + 128], (128, 128)
        ).T
    lanes = lax.broadcasted_iota(jnp.int32, (TILE, 128), 1).astype(f32)

    def step(i, carry):
        rows = pl.ds(pl.multiple_of(i * TILE, TILE), TILE)
        aim, lse = target[rows, :], row_lse[rows, :]
        for g, (h, at) in enumerate(lane_groups()):
            t = sv[h, rows, at]
            e = 0.5 * (jnp.exp2(t - lse) + jnp.exp2(t - cols_lse[:, g * 128 : g * 128 + 128]))
            slope[h, rows, at] = jnp.where(lanes == aim - g * 128, e - 1.0, e).astype(bf16)
        return carry

    lax.fori_loop(0, 1024 // TILE, step, 0, unroll=2)


def grad_kernel(flip, order, n_parts, n_ties, *refs):
    n = len(order)
    steps = [(g, i, d) for g, group in enumerate(order) for i, d in enumerate(group)]
    (slope, qt, pt), parts, refs = refs[:3], refs[3 : 3 + n_parts], refs[3 + n_parts + n_ties :]
    keeps, sends, (part_out, gq, gp, zeros, out_sems) = refs[:n], refs[n : 2 * n], refs[2 * n :]
    part_out[...] = sum((p[...] for p in parts), jnp.zeros((8, 128), f32))
    y, core, z, x = place()
    zeros[...] = jnp.zeros(zeros.shape, bf16)
    half = (x % 2) ^ flip
    rank = (x // 2) ^ flip
    whole = len(steps) == 4

    def q_rows(k, d):
        return (z + d) % 4 * 128 if whole else k * 128

    def p_rows(k, d):
        return (y + d) % 4 * 256 if whole else k * 256

    def slope_rows(h):
        if whole:
            return slope[h, pl.ds(pl.multiple_of(half * 512, 512), 512), :]
        starts = [pl.multiple_of(half * 512 + (z + d) % 4 * 128, 128) for _, _, d in steps]
        return jnp.concatenate([slope[h, pl.ds(r, 128), :] for r in starts], axis=0)

    def q_flip_rows():
        if whole:
            return qt[...]
        starts = [pl.multiple_of((y + d) % 4 * 256, 256) for _, _, d in steps]
        return jnp.concatenate([qt[pl.ds(r, 256), :] for r in starts], axis=0)


    def send_queries(which):
        copies = []
        for k, (g, i, d) in enumerate(steps):
            to = (sends if which else keeps)[g].at[i]
            at = pl.ds(pl.multiple_of(q_rows(k, d), 128), 128)
            copies.append(pltpu.make_async_copy(gq.at[at], to.at[which], out_sems.at[k, 0]))
            copies.append(pltpu.make_async_copy(zeros, to.at[1 - which], out_sems.at[k, 1]))
        return copies

    def send_passages(which, m, cut):
        copies = []
        for k, (g, i, d) in enumerate(steps):
            to = (keeps if which else sends)[g].at[i]
            for part in range(2):
                at = pl.ds(pl.multiple_of(p_rows(k, d) + (1 - part) * 128, 128), 128)
                copies.append(
                    pltpu.make_async_copy(gp.at[at, cut], to.at[part, :, cut], out_sems.at[k, 2 + 2 * m + part])
                )
        return copies

    def start(make):
        for which in range(2):

            @pl.when(core == which)
            def _():
                for copy in make(which):
                    copy.start()

    for m in range(4):
        cut = slice(m * 256, m * 256 + 256)
        g = sum(
            lax.dot_general(
                slope_rows(h), pt[h, cut, :], (((1,), (1,)), ((), ())), preferred_element_type=f32
            )
            for h in range(2)
        )
        gq[:, cut] = (logit_scale * g).astype(bf16)
    start(send_queries)
    cuts = [slice(m * 512, m * 512 + 512) for m in range(2)]
    for m, cut in enumerate(cuts):
        g = jnp.dot(q_flip_rows(), slope[rank, :, cut], preferred_element_type=f32)
        gp[:, cut] = (logit_scale * g).astype(bf16)
        start(functools.partial(send_passages, m=m, cut=cut))

    for which in range(2):

        @pl.when(core == which)
        def _():
            for copy in send_queries(which) + [c for m, cut in enumerate(cuts) for c in send_passages(which, m, cut)]:
                copy.wait()


ANY = pl.BlockSpec(memory_space=pl.ANY)
VM = pl.BlockSpec(memory_space=pltpu.VMEM)


def arr(shape, dtype):
    return jax.ShapeDtypeStruct(shape, dtype)


def cost(flops, nbytes):
    return pl.CostEstimate(flops=flops, bytes_accessed=nbytes, transcendentals=0)


def scores_of(mine, theirs, target):
    return pl.pallas_call(
        score_kernel,
        out_shape=(
            arr((2, 1024, 1024), f32),
            arr((3, 2048), f32),
            arr((3, 2048), f32),
            arr((1024, 1024), bf16),
            arr((2, 1024, 1024), bf16),
        ),
        in_specs=[ANY] * 16 + [VM],
        out_specs=(VM,) * 5,
        scratch_shapes=[
            pltpu.VMEM((1024, 128), f32),
            pltpu.VMEM((1024, 128), f32),
            pltpu.VMEM((2, 8, 1024), f32),
            pltpu.SemaphoreType.DMA((8, 3)),
        ],
        compiler_params=pltpu.CompilerParams(vmem_limit_bytes=18 * MIB),
        cost_estimate=cost(2 * 1024**2 * 2048, 16 * MIB),
        name="scores",
    )(*mine, *theirs, target)


def flip_kernel(q, out):
    for m in range(8):
        out[:, m * 128 : m * 128 + 128] = q[m * 128 : m * 128 + 128, :].T


def flipped(q):
    return pl.pallas_call(
        flip_kernel,
        out_shape=arr(q.shape, bf16),
        in_specs=[VM],
        out_specs=VM,
        compiler_params=pltpu.CompilerParams(vmem_limit_bytes=8 * MIB),
        cost_estimate=cost(0, 4 * MIB),
        name="flip",
    )(q)


def entry_kernel(q_in, p_in, mine, send, q, p, sems):
    copies = [pltpu.make_async_copy(q_in, q, sems.at[0]), pltpu.make_async_copy(p_in, p, sems.at[1])]
    for copy in copies:
        copy.start()
    for copy in copies:
        copy.wait()
    first = place()[1] == 0
    flat = p[...].T
    mine[...] = jnp.where(first, q[...], flat)
    send[...] = jnp.where(first, flat, q[...])


def entry(q, p):
    return pl.pallas_call(
        entry_kernel,
        out_shape=[arr((128, 1024), bf16)] * 2,
        in_specs=[ANY] * 2,
        out_specs=[VM] * 2,
        scratch_shapes=[pltpu.VMEM(q.shape, bf16), pltpu.VMEM(p.shape, bf16), pltpu.SemaphoreType.DMA((2,))],
        compiler_params=pltpu.CompilerParams(vmem_limit_bytes=4 * MIB),
        cost_estimate=cost(0, MIB),
        name="entry",
    )(q, p)


def aim_kernel(positive, out):
    _, _, z, x = place()
    side = (x + 1) % 4 // 2
    for s in range(8):
        p = positive[pl.ds(s % 4 * 4 + x // 2 * 2 + s // 4, 1), :]
        far_z, far_x = p >> 12, (p >> 10) & 3
        inside = (far_z == z) & ((((far_x + 1) & 3) >> 1) == side)
        aim = jnp.where(inside, (far_x >> 1) * 1024 + (p & 1023), -1).astype(f32)
        out[s * 128 : s * 128 + 128, :] = jnp.broadcast_to(aim, (128, 128)).T


def aims_of(positive):
    return pl.pallas_call(
        aim_kernel,
        out_shape=arr((1024, 128), f32),
        in_specs=[VM],
        out_specs=VM,
        compiler_params=pltpu.CompilerParams(vmem_limit_bytes=4 * MIB),
        cost_estimate=cost(0, MIB),
        name="aims",
    )(positive.reshape(16, 128))


def after_kernel(a, *refs):
    refs[-1][...] = a[...]


def after(a, *ties):
    return pl.pallas_call(
        after_kernel,
        out_shape=arr(a.shape, a.dtype),
        in_specs=[VM] + [ANY] * len(ties),
        out_specs=VM,
        compiler_params=pltpu.CompilerParams(vmem_limit_bytes=4 * MIB),
        cost_estimate=cost(0, 1024),
        name="after",
    )(a, *ties)


def finish_kernel(mine, other, grad_queries, grad_passages):
    first = place()[1] == 0
    a, b = mine[...], other[...]
    grad_queries[...] = jnp.where(first, a, b)
    grad_passages[...] = jnp.where(first, b, a).T


def finish(mine, other):
    return pl.pallas_call(
        finish_kernel,
        out_shape=[arr((128, 1024), f32), arr((1024, 128), f32)],
        in_specs=[VM] * 2,
        out_specs=[VM] * 2,
        compiler_params=pltpu.CompilerParams(vmem_limit_bytes=8 * MIB),
        cost_estimate=cost(0, 2 * MIB),
        name="finish",
    )(mine, other)


def slope_of(scores, target, own_lse, got_lse):
    return pl.pallas_call(
        slope_kernel,
        out_shape=arr((2, 1024, 1024), bf16),
        in_specs=[VM] * 4,
        out_specs=VM,
        scratch_shapes=[pltpu.VMEM((1024, 128), f32)],
        compiler_params=pltpu.CompilerParams(vmem_limit_bytes=8 * MIB),
        cost_estimate=cost(2 * 1024**2 * 2048, 12 * MIB),
        name="slope",
    )(scores, target, own_lse, got_lse)


def grads_of(flip, order, operands, parts, ties):
    n = sum(len(group) for group in order)
    operands = (*operands, *parts)
    chunks = [arr((len(group), 2, 128, 1024), bf16) for group in order]
    return pl.pallas_call(
        functools.partial(grad_kernel, flip, order, len(parts), len(ties)),
        out_shape=chunks * 2 + [arr((8, 128), f32)],
        in_specs=[VM] * len(operands) + [ANY] * len(ties),
        out_specs=[VM] * (2 * len(chunks) + 1),
        scratch_shapes=[
            pltpu.VMEM((n * 128, 1024), bf16),
            pltpu.VMEM((n * 256, 1024), bf16),
            pltpu.VMEM((128, 1024), bf16),
            pltpu.SemaphoreType.DMA((n, 6)),
        ],
        compiler_params=pltpu.CompilerParams(vmem_limit_bytes=12 * MIB),
        cost_estimate=cost(n * 1024**3, n * 5 * MIB),
        name="grads_far" if flip else "grads_near",
    )(*operands, *ties)


def join_kernel(picks, *refs):
    out = refs[-1]
    parts = [r[...] if p is None else r[p : p + 1] for p, r in zip(picks, refs)]
    out[...] = sum(p.astype(f32) for p in parts).astype(bf16)


def join(terms, ties=(), pick=None):
    a, n = terms[0], len(terms)
    return pl.pallas_call(
        functools.partial(join_kernel, [None] * (n - 1) + [pick]),
        out_shape=arr(a.shape, bf16),
        in_specs=[VM] * n + [ANY] * len(ties),
        out_specs=VM,
        compiler_params=pltpu.CompilerParams(vmem_limit_bytes=8 * MIB),
        cost_estimate=cost(a.size, 6 * a.size),
        name="join",
    )(*terms, *ties)


def total_kernel(n, *refs):
    mine, other = refs[-2:]
    mine[...] = sum(r[0, 0].astype(f32) for r in refs[:n])
    other[...] = sum(r[0, 1].astype(f32) for r in refs[:n])


def total(terms, ties=()):
    return pl.pallas_call(
        functools.partial(total_kernel, len(terms)),
        out_shape=[arr((128, 1024), f32)] * 2,
        in_specs=[VM] * len(terms) + [ANY] * len(ties),
        out_specs=[VM] * 2,
        compiler_params=pltpu.CompilerParams(vmem_limit_bytes=8 * MIB),
        cost_estimate=cost(5 * 2**18, 4 * MIB),
        name="total",
    )(*terms, *ties)


def merge_kernel(n, last, *refs):
    ins = refs[:n]
    top = ins[0][0:1]
    for a in ins[1:]:
        top = jnp.maximum(top, a[0:1])
    total = sum(a[1:2] * jnp.exp2(a[0:1] - top) for a in ins)
    hits = sum(a[2:3] for a in ins)
    if last:
        lse, part = refs[-2:]
        lse[...] = top + jnp.log2(total)
        figure = jnp.sum(lse[...] - 2.0 * hits, axis=1, keepdims=True)
        part[...] = jnp.broadcast_to(figure, (8, 128))
    else:
        out = refs[-1]
        out[0:1] = top
        out[1:2] = total
        out[2:3] = hits


def merge(ins, ties=(), last=False):
    return pl.pallas_call(
        functools.partial(merge_kernel, len(ins), last),
        out_shape=[arr((1, 2048), f32), arr((8, 128), f32)] if last else arr((3, 2048), f32),
        in_specs=[VM] * len(ins) + [ANY] * len(ties),
        out_specs=[VM, VM] if last else VM,
        compiler_params=pltpu.CompilerParams(vmem_limit_bytes=4 * MIB),
        cost_estimate=cost(0, 2**16),
        name="merge",
    )(*ins, *ties)


def shards(queries, passages, positive):
    mine, send = entry(queries, passages)
    own = jnp.stack([mine, swap(send)])
    down, up, far = hop(own, 3, False), hop(own, 1, False), hop(own, 2, False)
    across = hop(own, 0, True)
    down_across, up_across = hop(down, 0, True), hop(up, 0, True)
    far_across = hop(across, 2, False)
    chunks = [down_across, far_across, far, own, across, up_across, down, up]
    others = [swap(c) for c in chunks]

    target = aims_of(positive)
    scores, keep, send, q_tile, p_tile = scores_of(chunks, others, target)
    q_flip = flipped(q_tile)
    stats = merge([keep, swap(send)])
    stats = merge([stats, hop(stats, 0, True)], (q_flip,))
    own_lse, part = merge([stats, hop(stats, 2, False), hop(stats, 1, False), hop(stats, 3, False)], last=True)
    slope = slope_of(scores, target, own_lse, swap(own_lse))

    tiles = (slope, q_flip, p_tile)
    outs = grads_of(1, ((1, 3),), tiles, (part, hop_xor(part, 1)), ())
    sides, part = join([outs[0], swap(outs[1])]), outs[2]
    outs = grads_of(1, ((2,), (0,)), tiles, (part,), ())
    beyond, across, part = join([outs[0], swap(outs[2])]), [outs[1], swap(outs[3])], outs[4]
    ready = (sides, beyond)
    moved = hop(after(part, ready[0]), 2, False, 1)
    sides, beyond = hop(sides, 0, True), hop(beyond, 2, False)
    outs = grads_of(0, ((2,), (0,)), tiles, (part, moved), ready)
    far = join([outs[0], swap(outs[2])])
    home = join([outs[1], swap(outs[3])])
    outs = grads_of(0, ((1,), (3,)), tiles, (outs[4],), ())
    part = outs[4]
    up = join([outs[0], swap(outs[2]), sides], (), pick=0)
    down = join([outs[1], swap(outs[3]), sides], (), pick=1)
    across = hop(join([*across, beyond], ()), 0, True)
    far, up, down = hop(far, 2, False), hop(up, 1, False), hop(down, 3, False)
    part = after(part, far)
    part = part + hop(part, 0, True, 1)
    part = part + swap(part)
    mine, other = total([home, far, across, up, down], (part,))
    grad_queries, grad_passages = finish(mine, swap(other))
    loss = part[0, 0] / (32768.0 * log2_e)
    return loss, grad_queries, grad_passages


def solution(mesh):
    in_specs = (P(("row", "col"), None), P("col", "row"), P("row"))
    out_specs = (P(), P(("row", "col"), None), P("col", "row"))
    return jax.shard_map(shards, mesh=mesh, in_specs=in_specs, out_specs=out_specs, check_vma=False)
```

```python
import functools

import jax
import jax.numpy as jnp
from jax import lax
from jax.experimental import pallas as pl
from jax.experimental.pallas import tpu as pltpu
from jax.sharding import PartitionSpec as P

logit_scale = 40.0
log2_e = 1.4426950408889634
score_scale = logit_scale * log2_e
low = -1e30
AX = ("row", "col")
f32, bf16 = jnp.float32, jnp.bfloat16
MIB = 1024 * 1024


def lin(y, c, z, x):
    return ((y * 2 + c) * 4 + z) * 4 + x


def moves(step, turn):
    pairs = []
    for y in range(4):
        for z in range(4):
            for x in range(4):
                far_z, side = step(z, x, x ^ 1)
                pairs.append((lin(y, turn, z, x), lin(y, turn, far_z, side)))
                far_y, side = step(y, x, 3 - x)
                pairs.append((lin(y, 1 - turn, z, x), lin(far_y, 1 - turn, z, side)))
    return pairs


def hop(a, d, flip, turn=0):
    return lax.ppermute(a, AX, moves(lambda r, x, other: ((r + d) % 4, other if flip else x), turn))


def hop_xor(a, turn=0):
    return lax.ppermute(a, AX, moves(lambda r, x, other: (r ^ 1, x), turn))


def swap(a):
    return lax.ppermute(a, "row", [(i, i ^ 1) for i in range(8)])


def place():
    row, col = lax.axis_index("row"), lax.axis_index("col")
    return row // 2, row % 2, col // 4, col % 4


OFFSETS = [(3, 1), (2, 1), (2, 0), (0, 0), (0, 1), (1, 1), (3, 0), (1, 0)]


def load_copies(core, y, z, x, mine, theirs, q_dst, p_dst, sems):
    out = []
    for k, (d, flip) in enumerate(OFFSETS):
        slot = ((x % 2) ^ flip) * 4 + (z - d + 4) % 4
        far_y = (y - d + 4) % 4
        rank = (x // 2) ^ flip
        for which in range(2):
            copies = []
            q_src, p_src = (mine[k], theirs[k]) if which == 0 else (theirs[k], mine[k])
            if q_dst is not None:
                rows = pl.ds(pl.multiple_of(slot * 128, 128), 128)
                copies.append(pltpu.make_async_copy(q_src.at[which], q_dst.at[rows], sems.at[k, 0]))
            if p_dst is not None:
                for part in range(2):
                    rows = pl.ds(pl.multiple_of(far_y * 256 + (1 - part) * 128, 128), 128)
                    copies.append(
                        pltpu.make_async_copy(p_src.at[part], p_dst.at[rank, rows], sems.at[k, 1 + part])
                    )
            out.append((which, copies))
    return out


def run_copies(core, groups, start):
    for which in range(2):

        @pl.when(core == which)
        def _():
            for w, copies in groups:
                if w == which:
                    for copy in copies:
                        copy.start() if start else copy.wait()


TILE = 32


def lane_groups():
    return [(g // 8, slice(g % 8 * 128, g % 8 * 128 + 128)) for g in range(16)]


def fold(a):
    return sum(a[r : r + 8] for r in range(0, a.shape[0], 8))


def score_kernel(*refs):
    mine, theirs, (target, sv, keep, send, qv, pt, row_top, row_sum, col_top, sems) = (
        refs[:8],
        refs[8:16],
        refs[16:],
    )
    y, core, z, x = place()
    groups = load_copies(core, y, z, x, mine, theirs, qv, pt, sems)
    flips = [flip for _, flip in OFFSETS for _ in range(2)]
    early = [(w, c[:1] if flip else c) for flip, (w, c) in zip(flips, groups)]
    late = [(w, c[1:]) for flip, (w, c) in zip(flips, groups) if flip]
    run_copies(core, early, True)
    run_copies(core, late, True)
    for flip, copies in enumerate((early, late)):
        run_copies(core, copies, False)
        h = (x // 2) ^ flip
        for n in range(2):
            cols = slice(n * 512, n * 512 + 512)
            s = score_scale * jnp.dot(qv[...], pt[h, :, cols], preferred_element_type=f32)
            sv[h, :, cols] = s
            col_top[h, :, cols] = jnp.broadcast_to(jnp.max(s, axis=0, keepdims=True), (8, 512))
            top = jnp.maximum(
                jnp.maximum(s[:, :128], s[:, 128:256]), jnp.maximum(s[:, 256:384], s[:, 384:])
            )
            row_top[...] = top if flip == n == 0 else jnp.maximum(row_top[...], top)
    tops = []
    for s in range(8):
        rows = slice(s * 128, s * 128 + 128)
        top = jnp.max(row_top[rows, :].T, axis=0, keepdims=True)
        tops.append(top)
        row_top[rows, :] = jnp.broadcast_to(top, (128, 128)).T
    lanes = lax.broadcasted_iota(jnp.int32, (TILE, 128), 1).astype(f32)

    def step(i, carry):
        col_acc, hits = carry
        rows = pl.ds(pl.multiple_of(i * TILE, TILE), TILE)
        top, aim = row_top[rows, :], target[rows, :]
        total, cols = jnp.zeros((TILE, 128), f32), []
        for g, (h, at) in enumerate(lane_groups()):
            t = sv[h, rows, at]
            total = total + jnp.exp2(t - top)
            cols.append(col_acc[g] + fold(jnp.exp2(t - col_top[h, 0:1, at])))
            hits = hits + fold(jnp.where(lanes == aim - g * 128, t, 0.0))
        row_sum[rows, :] = total
        return tuple(cols), hits

    zero = jnp.zeros((8, 128), f32)
    col_acc, hits = lax.fori_loop(0, 1024 // TILE, step, ((zero,) * 16, zero), unroll=2)
    hits = jnp.sum(hits, axis=0, keepdims=True)

    def fill(rows_ref, cols_ref, first):
        off = 0 if first else 1024
        for s in range(8):
            at = slice(off + s * 128, off + s * 128 + 128)
            rows_ref[0:1, at] = tops[s]
            rows_ref[1:2, at] = jnp.sum(row_sum[s * 128 : s * 128 + 128, :].T, axis=0, keepdims=True)
        gap = slice(1024 - off, 2048 - off)
        rows_ref[0:1, gap] = jnp.full((1, 1024), low, f32)
        rows_ref[1:2, gap] = jnp.zeros((1, 1024), f32)
        rows_ref[2:3, :] = jnp.zeros((1, 2048), f32)
        rows_ref[2:3, :128] = hits
        for h in range(2):
            cols_ref[0:1, h * 1024 : h * 1024 + 1024] = col_top[h, 0:1, :]
        for g in range(16):
            cols_ref[1:2, g * 128 : g * 128 + 128] = jnp.sum(col_acc[g], axis=0, keepdims=True)
        cols_ref[2:3, :] = jnp.zeros((1, 2048), f32)

    @pl.when(core == 0)
    def _():
        fill(keep, send, True)

    @pl.when(core == 1)
    def _():
        fill(send, keep, False)


def slope_kernel(sv, target, own_lse, got_lse, slope, row_lse):
    first = place()[1] == 0
    mine_lse, their_lse = own_lse[...], got_lse[...]
    rows_lse = jnp.where(first, mine_lse[:, :1024], their_lse[:, 1024:])
    cols_lse = jnp.where(first, their_lse, mine_lse)
    for s in range(8):
        row_lse[s * 128 : s * 128 + 128, :] = jnp.broadcast_to(
            rows_lse[:, s * 128 : s * 128 + 128], (128, 128)
        ).T
    lanes = lax.broadcasted_iota(jnp.int32, (TILE, 128), 1).astype(f32)

    def step(i, carry):
        rows = pl.ds(pl.multiple_of(i * TILE, TILE), TILE)
        aim, lse = target[rows, :], row_lse[rows, :]
        for g, (h, at) in enumerate(lane_groups()):
            t = sv[h, rows, at]
            e = 0.5 * (jnp.exp2(t - lse) + jnp.exp2(t - cols_lse[:, g * 128 : g * 128 + 128]))
            slope[h, rows, at] = jnp.where(lanes == aim - g * 128, e - 1.0, e).astype(bf16)
        return carry

    lax.fori_loop(0, 1024 // TILE, step, 0, unroll=2)


def grad_kernel(flip, order, n_parts, n_ties, *refs):
    n = len(order)
    steps = [(g, i, d) for g, group in enumerate(order) for i, d in enumerate(group)]
    (slope, qt, pt), parts, refs = refs[:3], refs[3 : 3 + n_parts], refs[3 + n_parts + n_ties :]
    keeps, sends, (part_out, gq, gp, zeros, out_sems) = refs[:n], refs[n : 2 * n], refs[2 * n :]
    part_out[...] = sum((p[...] for p in parts), jnp.zeros((8, 128), f32))
    y, core, z, x = place()
    zeros[...] = jnp.zeros(zeros.shape, bf16)
    half = (x % 2) ^ flip
    rank = (x // 2) ^ flip
    whole = len(steps) == 4

    def q_rows(k, d):
        return (z + d) % 4 * 128 if whole else k * 128

    def p_rows(k, d):
        return (y + d) % 4 * 256 if whole else k * 256

    def slope_rows(h):
        if whole:
            return slope[h, pl.ds(pl.multiple_of(half * 512, 512), 512), :]
        starts = [pl.multiple_of(half * 512 + (z + d) % 4 * 128, 128) for _, _, d in steps]
        return jnp.concatenate([slope[h, pl.ds(r, 128), :] for r in starts], axis=0)

    def q_flip_rows():
        if whole:
            return qt[...]
        starts = [pl.multiple_of((y + d) % 4 * 256, 256) for _, _, d in steps]
        return jnp.concatenate([qt[pl.ds(r, 256), :] for r in starts], axis=0)


    def send_queries(which):
        copies = []
        for k, (g, i, d) in enumerate(steps):
            to = (sends if which else keeps)[g].at[i]
            at = pl.ds(pl.multiple_of(q_rows(k, d), 128), 128)
            copies.append(pltpu.make_async_copy(gq.at[at], to.at[which], out_sems.at[k, 0]))
            copies.append(pltpu.make_async_copy(zeros, to.at[1 - which], out_sems.at[k, 1]))
        return copies

    def send_passages(which, m, cut):
        copies = []
        for k, (g, i, d) in enumerate(steps):
            to = (keeps if which else sends)[g].at[i]
            for part in range(2):
                at = pl.ds(pl.multiple_of(p_rows(k, d) + (1 - part) * 128, 128), 128)
                copies.append(
                    pltpu.make_async_copy(gp.at[at, cut], to.at[part, :, cut], out_sems.at[k, 2 + 2 * m + part])
                )
        return copies

    def start(make):
        for which in range(2):

            @pl.when(core == which)
            def _():
                for copy in make(which):
                    copy.start()

    for m in range(4):
        cut = slice(m * 256, m * 256 + 256)
        g = sum(
            lax.dot_general(
                slope_rows(h), pt[h, cut, :], (((1,), (1,)), ((), ())), preferred_element_type=f32
            )
            for h in range(2)
        )
        gq[:, cut] = (logit_scale * g).astype(bf16)
    start(send_queries)
    cuts = [slice(m * 512, m * 512 + 512) for m in range(2)]
    for m, cut in enumerate(cuts):
        g = jnp.dot(q_flip_rows(), slope[rank, :, cut], preferred_element_type=f32)
        gp[:, cut] = (logit_scale * g).astype(bf16)
        start(functools.partial(send_passages, m=m, cut=cut))

    for which in range(2):

        @pl.when(core == which)
        def _():
            for copy in send_queries(which) + [c for m, cut in enumerate(cuts) for c in send_passages(which, m, cut)]:
                copy.wait()


ANY = pl.BlockSpec(memory_space=pl.ANY)
VM = pl.BlockSpec(memory_space=pltpu.VMEM)


def arr(shape, dtype):
    return jax.ShapeDtypeStruct(shape, dtype)


def cost(flops, nbytes):
    return pl.CostEstimate(flops=flops, bytes_accessed=nbytes, transcendentals=0)


def scores_of(mine, theirs, target):
    return pl.pallas_call(
        score_kernel,
        out_shape=(
            arr((2, 1024, 1024), f32),
            arr((3, 2048), f32),
            arr((3, 2048), f32),
            arr((1024, 1024), bf16),
            arr((2, 1024, 1024), bf16),
        ),
        in_specs=[ANY] * 16 + [VM],
        out_specs=(VM,) * 5,
        scratch_shapes=[
            pltpu.VMEM((1024, 128), f32),
            pltpu.VMEM((1024, 128), f32),
            pltpu.VMEM((2, 8, 1024), f32),
            pltpu.SemaphoreType.DMA((8, 3)),
        ],
        compiler_params=pltpu.CompilerParams(vmem_limit_bytes=18 * MIB),
        cost_estimate=cost(2 * 1024**2 * 2048, 16 * MIB),
        name="scores",
    )(*mine, *theirs, target)


def flip_kernel(q, out):
    for m in range(8):
        out[:, m * 128 : m * 128 + 128] = q[m * 128 : m * 128 + 128, :].T


def flipped(q):
    return pl.pallas_call(
        flip_kernel,
        out_shape=arr(q.shape, bf16),
        in_specs=[VM],
        out_specs=VM,
        compiler_params=pltpu.CompilerParams(vmem_limit_bytes=8 * MIB),
        cost_estimate=cost(0, 4 * MIB),
        name="flip",
    )(q)


def entry_kernel(q_in, p_in, mine, send, q, p, sems):
    copies = [pltpu.make_async_copy(q_in, q, sems.at[0]), pltpu.make_async_copy(p_in, p, sems.at[1])]
    for copy in copies:
        copy.start()
    for copy in copies:
        copy.wait()
    first = place()[1] == 0
    flat = p[...].T
    mine[...] = jnp.where(first, q[...], flat)
    send[...] = jnp.where(first, flat, q[...])


def entry(q, p):
    return pl.pallas_call(
        entry_kernel,
        out_shape=[arr((128, 1024), bf16)] * 2,
        in_specs=[ANY] * 2,
        out_specs=[VM] * 2,
        scratch_shapes=[pltpu.VMEM(q.shape, bf16), pltpu.VMEM(p.shape, bf16), pltpu.SemaphoreType.DMA((2,))],
        compiler_params=pltpu.CompilerParams(vmem_limit_bytes=4 * MIB),
        cost_estimate=cost(0, MIB),
        name="entry",
    )(q, p)


def aim_kernel(positive, out):
    _, _, z, x = place()
    side = (x + 1) % 4 // 2
    for s in range(8):
        p = positive[pl.ds(s % 4 * 4 + x // 2 * 2 + s // 4, 1), :]
        far_z, far_x = p >> 12, (p >> 10) & 3
        inside = (far_z == z) & ((((far_x + 1) & 3) >> 1) == side)
        aim = jnp.where(inside, (far_x >> 1) * 1024 + (p & 1023), -1).astype(f32)
        out[s * 128 : s * 128 + 128, :] = jnp.broadcast_to(aim, (128, 128)).T


def aims_of(positive):
    return pl.pallas_call(
        aim_kernel,
        out_shape=arr((1024, 128), f32),
        in_specs=[VM],
        out_specs=VM,
        compiler_params=pltpu.CompilerParams(vmem_limit_bytes=4 * MIB),
        cost_estimate=cost(0, MIB),
        name="aims",
    )(positive.reshape(16, 128))


def after_kernel(a, *refs):
    refs[-1][...] = a[...]


def after(a, *ties):
    return pl.pallas_call(
        after_kernel,
        out_shape=arr(a.shape, a.dtype),
        in_specs=[VM] + [ANY] * len(ties),
        out_specs=VM,
        compiler_params=pltpu.CompilerParams(vmem_limit_bytes=4 * MIB),
        cost_estimate=cost(0, 1024),
        name="after",
    )(a, *ties)


def finish_kernel(mine, other, grad_queries, grad_passages):
    first = place()[1] == 0
    a, b = mine[...], other[...]
    grad_queries[...] = jnp.where(first, a, b)
    grad_passages[...] = jnp.where(first, b, a).T


def finish(mine, other):
    return pl.pallas_call(
        finish_kernel,
        out_shape=[arr((128, 1024), f32), arr((1024, 128), f32)],
        in_specs=[VM] * 2,
        out_specs=[VM] * 2,
        compiler_params=pltpu.CompilerParams(vmem_limit_bytes=8 * MIB),
        cost_estimate=cost(0, 2 * MIB),
        name="finish",
    )(mine, other)


def slope_of(scores, target, own_lse, got_lse):
    return pl.pallas_call(
        slope_kernel,
        out_shape=arr((2, 1024, 1024), bf16),
        in_specs=[VM] * 4,
        out_specs=VM,
        scratch_shapes=[pltpu.VMEM((1024, 128), f32)],
        compiler_params=pltpu.CompilerParams(vmem_limit_bytes=8 * MIB),
        cost_estimate=cost(2 * 1024**2 * 2048, 12 * MIB),
        name="slope",
    )(scores, target, own_lse, got_lse)


def grads_of(flip, order, operands, parts, ties):
    n = sum(len(group) for group in order)
    operands = (*operands, *parts)
    chunks = [arr((len(group), 2, 128, 1024), bf16) for group in order]
    return pl.pallas_call(
        functools.partial(grad_kernel, flip, order, len(parts), len(ties)),
        out_shape=chunks * 2 + [arr((8, 128), f32)],
        in_specs=[VM] * len(operands) + [ANY] * len(ties),
        out_specs=[VM] * (2 * len(chunks) + 1),
        scratch_shapes=[
            pltpu.VMEM((n * 128, 1024), bf16),
            pltpu.VMEM((n * 256, 1024), bf16),
            pltpu.VMEM((128, 1024), bf16),
            pltpu.SemaphoreType.DMA((n, 6)),
        ],
        compiler_params=pltpu.CompilerParams(vmem_limit_bytes=12 * MIB),
        cost_estimate=cost(n * 1024**3, n * 5 * MIB),
        name="grads_far" if flip else "grads_near",
    )(*operands, *ties)


def join_kernel(picks, *refs):
    out = refs[-1]
    parts = [r[...] if p is None else r[p : p + 1] for p, r in zip(picks, refs)]
    out[...] = sum(p.astype(f32) for p in parts).astype(bf16)


def join(terms, ties=(), pick=None):
    a, n = terms[0], len(terms)
    return pl.pallas_call(
        functools.partial(join_kernel, [None] * (n - 1) + [pick]),
        out_shape=arr(a.shape, bf16),
        in_specs=[VM] * n + [ANY] * len(ties),
        out_specs=VM,
        compiler_params=pltpu.CompilerParams(vmem_limit_bytes=8 * MIB),
        cost_estimate=cost(a.size, 6 * a.size),
        name="join",
    )(*terms, *ties)


def total_kernel(n, *refs):
    mine, other = refs[-2:]
    mine[...] = sum(r[0, 0].astype(f32) for r in refs[:n])
    other[...] = sum(r[0, 1].astype(f32) for r in refs[:n])


def total(terms, ties=()):
    return pl.pallas_call(
        functools.partial(total_kernel, len(terms)),
        out_shape=[arr((128, 1024), f32)] * 2,
        in_specs=[VM] * len(terms) + [ANY] * len(ties),
        out_specs=[VM] * 2,
        compiler_params=pltpu.CompilerParams(vmem_limit_bytes=8 * MIB),
        cost_estimate=cost(5 * 2**18, 4 * MIB),
        name="total",
    )(*terms, *ties)


def merge_kernel(n, last, *refs):
    ins = refs[:n]
    top = ins[0][0:1]
    for a in ins[1:]:
        top = jnp.maximum(top, a[0:1])
    total = sum(a[1:2] * jnp.exp2(a[0:1] - top) for a in ins)
    hits = sum(a[2:3] for a in ins)
    if last:
        lse, part = refs[-2:]
        lse[...] = top + jnp.log2(total)
        figure = jnp.sum(lse[...] - 2.0 * hits, axis=1, keepdims=True)
        part[...] = jnp.broadcast_to(figure, (8, 128))
    else:
        out = refs[-1]
        out[0:1] = top
        out[1:2] = total
        out[2:3] = hits


def merge(ins, ties=(), last=False):
    return pl.pallas_call(
        functools.partial(merge_kernel, len(ins), last),
        out_shape=[arr((1, 2048), f32), arr((8, 128), f32)] if last else arr((3, 2048), f32),
        in_specs=[VM] * len(ins) + [ANY] * len(ties),
        out_specs=[VM, VM] if last else VM,
        compiler_params=pltpu.CompilerParams(vmem_limit_bytes=4 * MIB),
        cost_estimate=cost(0, 2**16),
        name="merge",
    )(*ins, *ties)


def shards(queries, passages, positive):
    mine, send = entry(queries, passages)
    own = jnp.stack([mine, swap(send)])
    down, up, far = hop(own, 3, False), hop(own, 1, False), hop(own, 2, False)
    across = hop(own, 0, True)
    down_across, up_across = hop(down, 0, True), hop(up, 0, True)
    far_across = hop(across, 2, False)
    chunks = [down_across, far_across, far, own, across, up_across, down, up]
    others = [swap(c) for c in chunks]

    target = aims_of(positive)
    scores, keep, send, q_tile, p_tile = scores_of(chunks, others, target)
    q_flip = flipped(q_tile)
    stats = merge([keep, swap(send)])
    stats = merge([stats, hop(stats, 0, True)], (q_flip,))
    own_lse, part = merge([stats, hop(stats, 2, False), hop(stats, 1, False), hop(stats, 3, False)], last=True)
    slope = slope_of(scores, target, own_lse, swap(own_lse))

    tiles = (slope, q_flip, p_tile)
    outs = grads_of(1, ((1, 3),), tiles, (part, hop_xor(part, 1)), ())
    sides, part = join([outs[0], swap(outs[1])]), outs[2]
    outs = grads_of(1, ((2,), (0,)), tiles, (part,), ())
    beyond, across, part = join([outs[0], swap(outs[2])]), [outs[1], swap(outs[3])], outs[4]
    ready = (sides, beyond)
    moved = hop(after(part, ready[0]), 2, False, 1)
    sides, beyond = hop(sides, 0, True), hop(beyond, 2, False)
    outs = grads_of(0, ((2,), (0,)), tiles, (part, moved), ready)
    far = join([outs[0], swap(outs[2])])
    home = join([outs[1], swap(outs[3])])
    outs = grads_of(0, ((1,), (3,)), tiles, (outs[4],), ())
    part = outs[4]
    up = join([outs[0], swap(outs[2]), sides], (), pick=0)
    down = join([outs[1], swap(outs[3]), sides], (), pick=1)
    across = hop(join([*across, beyond], ()), 0, True)
    far, up, down = hop(far, 2, False), hop(up, 1, False), hop(down, 3, False)
    part = after(part, far)
    part = part + hop(part, 0, True, 1)
    part = part + swap(part)
    mine, other = total([home, far, across, up, down], (part,))
    grad_queries, grad_passages = finish(mine, swap(other))
    loss = part[0, 0] / (32768.0 * log2_e)
    return loss, grad_queries, grad_passages


def solution(mesh):
    in_specs = (P(("row", "col"), None), P("col", "row"), P("row"))
    out_specs = (P(), P(("row", "col"), None), P("col", "row"))
    return jax.shard_map(shards, mesh=mesh, in_specs=in_specs, out_specs=out_specs, check_vma=False)
```
